256 devices in a mesh: problem: 16 (over x, y_hi, core), sample: 16 (over y_lo, z).
Axes of the slice: x: 4, y: 4 (y_hi: 2, y_lo: 2; y = y_hi * 2 + y_lo), z: 8, core: 2. Of those that a mesh axis runs over, the one named last changes fastest.
Arguments:
- queries: bfloat16 [256, 256, 1024], P(('problem', 'sample')), parts along dimension 0, may hold values from -6 to 6
- resp_keys: bfloat16 [256, 256, 128], P(('problem', 'sample')), parts along dimension 0, may hold values from -6 to 6
- resp_values: bfloat16 [256, 256, 128], P(('problem', 'sample')), parts along dimension 0, may hold values from -6 to 6
- prompt_keys: bfloat16 [32768, 128], P(('problem', 'sample')), parts along dimension 0, may hold values from -6 to 6
- prompt_values: bfloat16 [32768, 128], P(('problem', 'sample')), parts along dimension 0, may hold values from -6 to 6
- grad_out: bfloat16 [256, 256, 1024], P(('problem', 'sample')), parts along dimension 0, may hold values from -24 to 24
- lengths: int32 [256], P(('problem', 'sample')), parts along dimension 0, may hold values from 64 to 256
- rewards: int32 [256], P(('problem', 'sample')), parts along dimension 0, may hold values from 0 to 16
Outputs:
- grad_queries: float32 [256, 256, 1024], P(('problem', 'sample')), parts along dimension 0
- grad_resp_keys: float32 [256, 256, 128], P(('problem', 'sample')), parts along dimension 0
- grad_resp_values: float32 [256, 256, 128], P(('problem', 'sample')), parts along dimension 0
- grad_prompt_keys: float32 [32768, 128], P(('problem', 'sample')), parts along dimension 0
- grad_prompt_values: float32 [32768, 128], P(('problem', 'sample')), parts along dimension 0
The draws below stay inside these ranges and needn't reach their ends.
There are 16 independent parts, one for each index of `problem`. The reference program is written for one: setup_inputs(seed, part) draws one part's arguments, and reference() takes and returns one part's arrays. A program takes and returns all parts, laid end to end along the dimension named above; each array names one. Nothing has to cross between parts.
All inputs are finite; a program needn't handle non-finite values.
Results may differ from the reference program's by a relative error of at most 0.007.
Values may be sent and summed in bfloat16 or wider, within the bound.
No kernel may reach another device: no remote copies, remote signals or barrier semaphores. Data moves between devices by JAX's collectives and lax.ppermute only.
A program may use at most 64 MiB of HBM per device.

```python
import jax
import jax.numpy as jnp
from jax import lax

HEADS = 8
HD = 128
RESP = 256
TESTS = 16
SAMPLES = 16
PROMPT = 2048


def draw_prompt_keys(key, part):
    key = jax.random.fold_in(key, 5)
    base = jax.random.normal(key, (PROMPT, HD), jnp.float32)
    base = jnp.clip(base, -6.0, 6.0)
    return base.astype(jnp.bfloat16)


def draw_queries(key, part):
    key = jax.random.fold_in(key, 9)
    base = jax.random.normal(key, (SAMPLES, RESP, HEADS, HD), jnp.float32)
    base = jnp.clip(base, -6.0, 6.0)
    return base.reshape(SAMPLES, RESP, HEADS * HD).astype(jnp.bfloat16)


def place_ends(values, own_key, smallest, largest):
    place = [jax.random.randint(jax.random.fold_in(own_key, axis), (), 0, length) for axis, length in enumerate(values.shape)]
    main_axis = values.shape.index(max(values.shape))
    beside = place[:main_axis] + [(place[main_axis] + 1) % values.shape[main_axis]] + place[main_axis + 1:]
    return values.at[tuple(place)].set(smallest).at[tuple(beside)].set(largest)


def block_levels(own_key, dims, shards, smallest, top_value):
    level = 1.0
    for axis_at, blocks in shards:
        draws = jax.random.uniform(jax.random.fold_in(jax.random.fold_in(own_key, 6), axis_at), (blocks,), jnp.float32, smallest / len(shards), top_value / len(shards))
        level = level * jnp.repeat(jnp.exp(draws), dims[axis_at] // blocks).reshape((-1,) + (1,) * (len(dims) - 1 - axis_at))
    return level


def gaussian(key, shape, deviation, most, cuts=(), dtype=jnp.bfloat16):
    values = deviation * jax.random.normal(key, shape, jnp.float32)
    if cuts:
        values = values * block_levels(key, shape, cuts, -0.22, 0.18)
    return jnp.clip(values, -most, most).astype(dtype)


def setup_inputs(seed: int = 0, part: int = 0) -> dict:
    splits = jax.random.split(jax.random.key(seed), 9)
    part_splits = jax.random.split(jax.random.fold_in(splits[8], part), 9)
    return {
        "queries": draw_queries(jax.random.fold_in(jax.random.fold_in(splits[8], part), 71), part),
        "resp_keys": gaussian(part_splits[1], (SAMPLES, RESP, HD), 1.0, 6.0, ((0, 16),)),
        "resp_values": gaussian(part_splits[2], (SAMPLES, RESP, HD), 1.0, 6.0, ((0, 16),)),
        "prompt_keys": draw_prompt_keys(jax.random.fold_in(jax.random.fold_in(splits[8], part), 71), part),
        "prompt_values": gaussian(part_splits[4], (PROMPT, HD), 1.0, 6.0, ((0, 16),)),
        "grad_out": gaussian(part_splits[5], (SAMPLES, RESP, HEADS * HD), 4.0, 24.0, ((0, 16),)),
        "lengths": place_ends(jax.random.randint(part_splits[6], (SAMPLES,), RESP // 4, RESP + 1), jax.random.fold_in(part_splits[6], 1), RESP // 4, RESP).astype(jnp.int32),
        "rewards": place_ends(jax.random.randint(part_splits[7], (SAMPLES,), 0, TESTS + 1), jax.random.fold_in(part_splits[7], 1), 0, TESTS).astype(jnp.int32),
    }


def one_sample(inputs, prompt_keys, prompt_values):
    queries, own_keys, own_values, grad_out, length = inputs
    query_count = RESP * HEADS
    score_scale = 1.0 / (HD ** 0.5)
    query_rows = queries.reshape(query_count, HD)
    all_keys = jnp.concatenate([prompt_keys, own_keys], axis=0)
    all_values = jnp.concatenate([prompt_values, own_values], axis=0)
    position = lax.broadcasted_iota(jnp.int32, (query_count, 1), 0) // HEADS
    column = lax.broadcasted_iota(jnp.int32, (1, PROMPT + RESP), 1) - PROMPT
    allowed = column <= position
    scores = jnp.dot(query_rows, all_keys.T, preferred_element_type=jnp.float32) * score_scale
    scores = jnp.where(allowed, scores, -jnp.inf)
    row_max = jnp.max(scores, axis=1, keepdims=True)
    logsum = row_max + jnp.log(jnp.sum(jnp.exp(scores - row_max), axis=1, keepdims=True))
    attention = jnp.exp(scores - logsum)
    rounded = attention.astype(jnp.bfloat16)
    attended = jnp.dot(rounded, all_values, preferred_element_type=jnp.float32)
    cotangent = jnp.where(position < length, grad_out.reshape(query_count, HD), jnp.zeros((), jnp.bfloat16))
    row_delta = jnp.sum(cotangent.astype(jnp.float32) * attended, axis=1, keepdims=True)
    slope_grad = jnp.dot(cotangent, all_values.T, preferred_element_type=jnp.float32)
    score_grad = (attention * (slope_grad - row_delta)).astype(jnp.bfloat16)
    query_grad = jnp.dot(score_grad, all_keys, preferred_element_type=jnp.float32) * score_scale
    key_grad = jnp.dot(score_grad.T, query_rows, preferred_element_type=jnp.float32) * score_scale
    value_grad = jnp.dot(rounded.T, cotangent, preferred_element_type=jnp.float32)
    return query_grad.reshape(RESP, HEADS * HD), key_grad, value_grad


def reference(queries, resp_keys, resp_values, prompt_keys, prompt_values, grad_out, lengths, rewards):
    reward_float = rewards.astype(jnp.float32)
    advantage = reward_float - jnp.sum(reward_float) / SAMPLES
    query_grad, key_grad, value_grad = lax.map(
        lambda inputs: one_sample(inputs, prompt_keys, prompt_values),
        (queries, resp_keys, resp_values, grad_out, lengths))
    scaled = advantage[:, None, None]
    prompt_key_grad = jnp.sum(scaled * key_grad[:, :PROMPT], axis=0)
    prompt_value_grad = jnp.sum(scaled * value_grad[:, :PROMPT], axis=0)
    return (scaled * query_grad, scaled * key_grad[:, PROMPT:], scaled * value_grad[:, PROMPT:],
            prompt_key_grad, prompt_value_grad)
```

```python
import functools
import math

import jax
import jax.numpy as jnp
from jax import lax
from jax.experimental import pallas as pl
from jax.experimental.pallas import tpu as pltpu
from jax.sharding import PartitionSpec as P

F32 = jnp.float32
BF16 = jnp.bfloat16
CHUNK = 256


def dot_nn(left, right):
    return lax.dot_general(left, right, (((1,), (0,)), ((), ())), preferred_element_type=F32)


def dot_nt(left, right):
    return lax.dot_general(left, right, (((1,), (1,)), ((), ())), preferred_element_type=F32)


def fold_rows(values, combine):
    parts = [values[i : i + 8] for i in range(0, values.shape[0], 8)]
    while len(parts) > 1:
        parts = [
            combine(parts[i], parts[i + 1]) if i + 1 < len(parts) else parts[i]
            for i in range(0, len(parts), 2)
        ]
    return parts[0]


def attention_kernel(
    heads, owners, share, len_ref, q_ref, c_ref, g_ref, rk_ref, rv_ref,
    dq_ref, drk_ref, drv_ref, dp_ref,
    k_all, v_all, k_t, dk_acc, dv_acc, s0, s1, g0, g1, g2, e0, e1,
):
    resp, width = rk_ref.shape[1], rk_ref.shape[2]
    prompt = owners * share
    keys = prompt + resp
    chunks = keys // CHUNK
    scale = 1.0 / math.sqrt(width)
    rate = scale * math.log2(math.e)
    s_buf, g_buf, e_buf = (s0, s1), (g0, g1, g2), (e0, e1)

    for owner in range(owners):
        rows = pl.ds(owner * share, share)
        k_all[rows, :] = g_ref[owner, :share, :]
        v_all[rows, :] = g_ref[owner, share : 2 * share, :]
    k_all[prompt:, :] = rk_ref[0]
    v_all[prompt:, :] = rv_ref[0]
    for j in range(chunks):
        span = slice(j * CHUNK, (j + 1) * CHUNK)
        k_t[:, span] = k_all[span, :].T

    total = jnp.zeros((1, width), F32)
    for owner in range(owners):
        total = total + g_ref[owner, 2 * share : 2 * share + 16, :].astype(F32)[:1]
    me = lax.axis_index("sample")
    mine = g_ref[me, 2 * share : 2 * share + 16, :].astype(F32)[:1]
    advantage = mine - total / owners

    live = lax.broadcasted_iota(jnp.int32, (resp, width), 0) < len_ref[0]
    allowed = lax.broadcasted_iota(jnp.int32, (CHUNK, resp), 0) <= lax.broadcasted_iota(
        jnp.int32, (CHUNK, resp), 1
    )

    def query_rows(h):
        return q_ref[0, :, h * width : (h + 1) * width]

    def cotangent(h):
        return jnp.where(live, c_ref[0, :, h * width : (h + 1) * width], jnp.zeros((), BF16))

    peak, inv, delta = {}, {}, {}
    for t in range(heads + 2):
        one, two, three = t, t - 1, t - 2
        do1, do2, do3 = one < heads, 0 <= two < heads, 0 <= three
        if do1:
            q1, c1 = query_rows(one), cotangent(one)
            top = None
        if do2:
            level = peak[two] * rate
            mass = mixed = None
        if do3:
            q3, c3 = query_rows(three), cotangent(three)
            dq_t = jnp.zeros((width, resp), F32)
        for j in range(chunks):
            span = slice(j * CHUNK, (j + 1) * CHUNK)
            if do1:
                s = dot_nt(k_all[span, :], q1)
                if j == chunks - 1:
                    s = jnp.where(allowed, s, -jnp.inf)
                s_buf[one % 2][span, :] = s
                part = fold_rows(s, jnp.maximum)
                top = part if top is None else jnp.maximum(top, part)
                g_buf[one % 3][span, :] = dot_nt(v_all[span, :], c1)
            if do2:
                e = jnp.exp2(s_buf[two % 2][span, :] * rate - level)
                e_buf[two % 2][span, :] = e
                part = fold_rows(e, jnp.add)
                mass = part if mass is None else mass + part
                part = fold_rows(e * g_buf[two % 3][span, :], jnp.add)
                mixed = part if mixed is None else mixed + part
            if do3:
                p = e_buf[three % 2][span, :] * inv[three]
                ds = (p * (g_buf[three % 3][span, :] - delta[three])).astype(BF16)
                dv = dot_nn(p.astype(BF16), c3)
                dk = dot_nn(ds, q3)
                if three == 0:
                    dv_acc[span, :] = dv
                    dk_acc[span, :] = dk
                else:
                    dv_acc[span, :] += dv
                    dk_acc[span, :] += dk
                dq_t = dq_t + dot_nn(k_t[:, span], ds)
        if do1:
            peak[one] = jnp.max(top, axis=0, keepdims=True)
        if do2:
            inv[two] = 1.0 / jnp.sum(mass, axis=0, keepdims=True)
            delta[two] = jnp.sum(mixed, axis=0, keepdims=True) * inv[two]
        if do3:
            dq_ref[0, :, three * width : (three + 1) * width] = dq_t.T * (advantage * scale)

    drk_ref[0] = dk_acc[prompt:, :] * (advantage * scale)
    drv_ref[0] = dv_acc[prompt:, :] * advantage
    for owner in range(owners):
        rows = pl.ds(owner * share, share)
        dp_ref[owner, :share, :] = (dk_acc[rows, :] * (advantage * scale)).astype(BF16)
        dp_ref[owner, share:, :] = (dv_acc[rows, :] * advantage).astype(BF16)


def attention_grads(lengths, queries, grad_out, gathered, resp_keys, resp_values):
    owners = gathered.shape[0]
    resp, width = resp_keys.shape[1:]
    heads = queries.shape[2] // width
    share = (gathered.shape[1] - 16) // 2
    keys = owners * share + resp
    vmem = pl.BlockSpec(memory_space=pltpu.VMEM)
    products = 5 * 2 * heads * resp * keys * width
    return pl.pallas_call(
        functools.partial(attention_kernel, heads, owners, share),
        out_shape=(
            jax.ShapeDtypeStruct(queries.shape, F32),
            jax.ShapeDtypeStruct(resp_keys.shape, F32),
            jax.ShapeDtypeStruct(resp_values.shape, F32),
            jax.ShapeDtypeStruct((owners, 2 * share, width), BF16),
        ),
        in_specs=[pl.BlockSpec(memory_space=pltpu.SMEM)] + [vmem] * 5,
        out_specs=(vmem,) * 4,
        scratch_shapes=[
            pltpu.VMEM((keys, width), BF16),
            pltpu.VMEM((keys, width), BF16),
            pltpu.VMEM((width, keys), BF16),
            pltpu.VMEM((keys, width), F32),
            pltpu.VMEM((keys, width), F32),
        ]
        + [pltpu.VMEM((keys, resp), F32)] * 7,
        compiler_params=pltpu.CompilerParams(vmem_limit_bytes=48 * 1024 * 1024),
        cost_estimate=pl.CostEstimate(
            flops=products, bytes_accessed=8 * 1024 * 1024, transcendentals=heads * resp * keys
        ),
        name="attention_grads",
    )(lengths, queries, grad_out, gathered, resp_keys, resp_values)


def shards(queries, resp_keys, resp_values, prompt_keys, prompt_values, grad_out, lengths, rewards):
    share, width = prompt_keys.shape
    reward_rows = jnp.broadcast_to(rewards.astype(BF16)[:, None], (16, width))
    packed = jnp.concatenate([prompt_keys, prompt_values, reward_rows], axis=0)
    gathered = lax.all_gather(packed, "sample", axis=0, tiled=False)
    grad_queries, grad_resp_keys, grad_resp_values, parts = attention_grads(
        lengths, queries, grad_out, gathered, resp_keys, resp_values
    )
    received = lax.all_to_all(parts, "sample", split_axis=0, concat_axis=0, tiled=True)
    summed = jnp.sum(received.astype(F32), axis=0)
    return grad_queries, grad_resp_keys, grad_resp_values, summed[:share], summed[share:]


def solution(mesh):
    whole = P(("problem", "sample"), None, None)
    rows = P(("problem", "sample"), None)
    one = P(("problem", "sample"))
    return jax.shard_map(
        shards,
        mesh=mesh,
        in_specs=(whole, whole, whole, rows, rows, whole, one, one),
        out_specs=(whole, whole, whole, rows, rows),
        check_vma=False,
    )
```

```python
import functools
import math

import jax
import jax.numpy as jnp
from jax import lax
from jax.experimental import pallas as pl
from jax.experimental.pallas import tpu as pltpu
from jax.sharding import PartitionSpec as P

F32 = jnp.float32
BF16 = jnp.bfloat16
PAD = 16
PIECES = 3
SLICE = 64


def dot_nn(left, right):
    return lax.dot_general(left, right, (((1,), (0,)), ((), ())), preferred_element_type=F32)


def dot_nt(left, right):
    return lax.dot_general(left, right, (((1,), (1,)), ((), ())), preferred_element_type=F32)


def fold_rows(values, combine):
    parts = [values[i : i + 8] for i in range(0, values.shape[0], 8)]
    while len(parts) > 1:
        parts = [
            combine(parts[i], parts[i + 1]) if i + 1 < len(parts) else parts[i]
            for i in range(0, len(parts), 2)
        ]
    return parts[0]


def attention_kernel(
    heads, owners, share, len_ref, pay_ref, q_hbm, c_hbm, g_hbm, rk_hbm, rv_hbm,
    dq_ref, drk_ref, drv_ref, dp_ref,
    q_rows, c_rows, k_all, v_all, pay, k_t, dk_acc, dv_acc,
    s0, s1, g0, g1, e0, e1, p0, p1, ds0, ds1, q_sems, c_sems, sems,
):
    resp, width = rk_hbm.shape[1], rk_hbm.shape[2]
    prompt = owners * share
    keys = prompt + resp
    piece = keys // PIECES
    per_piece = piece // share
    scale = 1.0 / math.sqrt(width)
    rate = scale * math.log2(math.e)
    s_buf, g_buf, e_buf = (s0, s1), (g0, g1), (e0, e1)
    p_buf, ds_buf = (p0, p1), (ds0, ds1)

    def head_rows(h):
        return pl.ds(h * resp, resp)

    bring_q, bring_c = [], []
    for h in range(heads):
        lanes = pl.ds(h * width, width)
        bring_q.append(
            pltpu.make_async_copy(q_hbm.at[0, :, lanes], q_rows.at[head_rows(h), :], q_sems.at[h])
        )
        bring_c.append(
            pltpu.make_async_copy(c_hbm.at[0, :, lanes], c_rows.at[head_rows(h), :], c_sems.at[h])
        )
    owned = resp // share
    moves = [
        (g_hbm.at[:, pl.ds(0, share), :], k_all.at[pl.ds(0, owners)]),
        (g_hbm.at[:, pl.ds(share, share), :], v_all.at[pl.ds(0, owners)]),
        (g_hbm.at[:, pl.ds(2 * share, PAD), :], pay),
    ]
    for i in range(owned):
        rows = pl.ds(i * share, share)
        moves.append((rk_hbm.at[0, rows, :], k_all.at[owners + i]))
        moves.append((rv_hbm.at[0, rows, :], v_all.at[owners + i]))
    bring = [pltpu.make_async_copy(src, dst, sems.at[i]) for i, (src, dst) in enumerate(moves)]
    bring_q[0].start()
    bring_c[0].start()
    for copy in bring:
        copy.start()
    for h in range(1, heads):
        bring_q[h].start()
        bring_c[h].start()
    for copy in bring:
        copy.wait()

    total = jnp.zeros((1, width), F32)
    for owner in range(owners):
        total = total + pay[owner].astype(F32)[:1]
    advantage = pay_ref[0].astype(F32) - total / owners

    live = lax.broadcasted_iota(jnp.int32, (resp, width), 0) < len_ref[0]
    key_at = lax.broadcasted_iota(jnp.int32, (SLICE, resp), 0)
    query_at = lax.broadcasted_iota(jnp.int32, (SLICE, resp), 1)

    def rows_of(ref, i):
        return ref[i * per_piece : (i + 1) * per_piece].reshape(piece, width)

    peaks, rescale, delta = {}, {}, {}
    for t in range(heads + 1):
        one, two = t, t - 1
        do1, do2 = one < heads, two >= 0
        if do1:
            bring_q[one].wait()
            bring_c[one].wait()
            rows = head_rows(one)
            q1 = q_rows[rows, :]
            c1 = jnp.where(live, c_rows[rows, :], jnp.zeros((), BF16))
            c_rows[rows, :] = c1
            mass = mixed = peak = None
            levels = []
        if do2:
            pair = (two // 2) % 2
            half = slice((two % 2) * resp, (two % 2 + 1) * resp)
            dq_t = None
        for i in range(PIECES):
            first = i * piece
            span = slice(first, first + piece)
            if t == 0:
                k_t[:, span] = rows_of(k_all, i).T
            if do1:
                s_now, g_now, e_now = s_buf[i % 2], g_buf[one % 2], e_buf[one % 2]
                s_now[...] = dot_nt(rows_of(k_all, i), q1)
                g_now[span, :] = dot_nt(rows_of(v_all, i), c1)
                top = None
                for at in range(0, piece, SLICE):
                    s = s_now[at : at + SLICE, :]
                    if first + at >= prompt:
                        s = jnp.where(key_at + (first + at - prompt) <= query_at, s, -jnp.inf)
                    part = fold_rows(s, jnp.maximum)
                    top = part if top is None else jnp.maximum(top, part)
                top = jnp.max(top, axis=0, keepdims=True)
                if peak is None:
                    peak = top
                    levels.append(peak * rate)
                else:
                    peak = jnp.maximum(peak, top)
                    levels.append(peak * rate)
                    weight = jnp.exp2(levels[-2] - levels[-1])
                    mass, mixed = mass * weight, mixed * weight
                for at in range(0, piece, SLICE):
                    e = jnp.exp2(s_now[at : at + SLICE, :] * rate - levels[-1])
                    if first + at >= prompt:
                        e = jnp.where(key_at + (first + at - prompt) <= query_at, e, 0.0)
                    e_now[first + at : first + at + SLICE, :] = e
                    part = fold_rows(e, jnp.add)
                    mass = part if mass is None else mass + part
                    part = fold_rows(e * g_now[first + at : first + at + SLICE, :], jnp.add)
                    mixed = part if mixed is None else mixed + part
            if do2:
                factor, shift = rescale[two][i], delta[two]
                for at in range(first, first + piece, SLICE):
                    here = slice(at, at + SLICE)
                    p = e_buf[two % 2][here, :] * factor
                    p_buf[pair][here, half] = p.astype(BF16)
                    ds_buf[pair][here, half] = (p * (g_buf[two % 2][here, :] - shift)).astype(BF16)
                part = dot_nn(k_t[:, span], ds_buf[pair][span, half])
                dq_t = part if dq_t is None else dq_t + part
                if two % 2 == 1:
                    both = slice((two - 1) * resp, (two + 1) * resp)
                    dk = dot_nn(ds_buf[pair][span, :], q_rows[both, :])
                    dv = dot_nn(p_buf[pair][span, :], c_rows[both, :])
                    if two > 1:
                        dk = dk_acc[span, :] + dk
                        dv = dv_acc[span, :] + dv
                    if two < heads - 1:
                        dk_acc[span, :] = dk
                        dv_acc[span, :] = dv
                    else:
                        dk = dk * (advantage * scale)
                        dv = dv * advantage
                        for sub in range(per_piece):
                            owner = i * per_piece + sub
                            part = slice(sub * share, (sub + 1) * share)
                            if owner < owners:
                                dp_ref[owner, :share, :] = dk[part].astype(BF16)
                                dp_ref[owner, share:, :] = dv[part].astype(BF16)
                            else:
                                rows = slice((owner - owners) * share, (owner - owners + 1) * share)
                                drk_ref[0, rows, :] = dk[part]
                                drv_ref[0, rows, :] = dv[part]
        if do1:
            inv = 1.0 / jnp.sum(mass, axis=0, keepdims=True)
            delta[one] = jnp.sum(mixed, axis=0, keepdims=True) * inv
            rescale[one] = [jnp.exp2(level - levels[-1]) * inv for level in levels]
        if do2:
            dq_ref[0, :, two * width : (two + 1) * width] = dq_t.T * (advantage * scale)


def attention_grads(lengths, rewards, queries, grad_out, gathered, resp_keys, resp_values):
    owners = gathered.shape[0]
    resp, width = resp_keys.shape[1:]
    heads = queries.shape[2] // width
    share = (gathered.shape[1] - PAD) // 2
    keys = owners * share + resp
    piece = keys // PIECES
    vmem = pl.BlockSpec(memory_space=pltpu.VMEM)
    smem = pl.BlockSpec(memory_space=pltpu.SMEM)
    return pl.pallas_call(
        functools.partial(attention_kernel, heads, owners, share),
        out_shape=(
            jax.ShapeDtypeStruct(queries.shape, F32),
            jax.ShapeDtypeStruct(resp_keys.shape, F32),
            jax.ShapeDtypeStruct(resp_values.shape, F32),
            jax.ShapeDtypeStruct((owners, 2 * share, width), BF16),
        ),
        in_specs=[smem] * 2 + [pl.BlockSpec(memory_space=pl.ANY)] * 5,
        out_specs=(vmem,) * 4,
        scratch_shapes=[
            pltpu.VMEM((heads * resp, width), BF16),
            pltpu.VMEM((heads * resp, width), BF16),
            pltpu.VMEM((keys // share, share, width), BF16),
            pltpu.VMEM((keys // share, share, width), BF16),
            pltpu.VMEM((owners, PAD, width), BF16),
            pltpu.VMEM((width, keys), BF16),
            pltpu.VMEM((keys, width), F32),
            pltpu.VMEM((keys, width), F32),
        ]
        + [pltpu.VMEM((piece, resp), F32)] * 2
        + [pltpu.VMEM((keys, resp), F32)] * 4
        + [pltpu.VMEM((keys, 2 * resp), BF16)] * 4
        + [
            pltpu.SemaphoreType.DMA((heads,)),
            pltpu.SemaphoreType.DMA((heads,)),
            pltpu.SemaphoreType.DMA((3 + 2 * (resp // share),)),
        ],
        compiler_params=pltpu.CompilerParams(vmem_limit_bytes=48 * 1024 * 1024),
        cost_estimate=pl.CostEstimate(
            flops=10 * heads * resp * keys * width,
            bytes_accessed=4 * 1024 * 1024,
            transcendentals=heads * resp * keys,
        ),
        name="attention_grads",
    )(lengths, rewards, queries, grad_out, gathered, resp_keys, resp_values)


def shards(queries, resp_keys, resp_values, prompt_keys, prompt_values, grad_out, lengths, rewards):
    share, width = prompt_keys.shape
    owners = lax.axis_size("sample")
    reward_rows = jnp.broadcast_to(rewards.astype(BF16)[:, None], (PAD, width))
    packed = jnp.concatenate([prompt_keys, prompt_values, reward_rows], axis=0)
    copies = jnp.broadcast_to(packed[None], (owners,) + packed.shape)
    gathered = lax.all_to_all(copies, "sample", split_axis=0, concat_axis=0, tiled=True)
    grad_queries, grad_resp_keys, grad_resp_values, parts = attention_grads(
        lengths, rewards, queries, grad_out, gathered, resp_keys, resp_values
    )
    received = lax.all_to_all(parts, "sample", split_axis=0, concat_axis=0, tiled=True)
    summed = jnp.sum(received.astype(F32), axis=0)
    return grad_queries, grad_resp_keys, grad_resp_values, summed[:share], summed[share:]


def solution(mesh):
    whole = P(("problem", "sample"), None, None)
    rows = P(("problem", "sample"), None)
    one = P(("problem", "sample"))
    return jax.shard_map(
        shards,
        mesh=mesh,
        in_specs=(whole, whole, whole, rows, rows, whole, one, one),
        out_specs=(whole, whole, whole, rows, rows),
        check_vma=False,
    )
```

```python
import functools
import math

import jax
import jax.numpy as jnp
from jax import lax
from jax.experimental import pallas as pl
from jax.experimental.pallas import tpu as pltpu
from jax.sharding import PartitionSpec as P

F32 = jnp.float32
BF16 = jnp.bfloat16
PAD = 16
RING = 8
SLICE = 64

VMEM_SPEC = pl.BlockSpec(memory_space=pltpu.VMEM)
SMEM_SPEC = pl.BlockSpec(memory_space=pltpu.SMEM)
ANY_SPEC = pl.BlockSpec(memory_space=pl.ANY)


def dot_nn(left, right):
    return lax.dot_general(left, right, (((1,), (0,)), ((), ())), preferred_element_type=F32)


def dot_nt(left, right):
    return lax.dot_general(left, right, (((1,), (1,)), ((), ())), preferred_element_type=F32)


def fold_rows(values, combine):
    parts = [values[i : i + 8] for i in range(0, values.shape[0], 8)]
    while len(parts) > 1:
        parts = [
            combine(parts[i], parts[i + 1]) if i + 1 < len(parts) else parts[i]
            for i in range(0, len(parts), 2)
        ]
    return parts[0]


def pack_places(blocks, share):
    size = 2 * share + PAD
    return [(ref, at) for ref in blocks for at in range(0, ref.shape[0], size)]


def load_rows(blocks, own, k_all, v_all, share):
    places = pack_places(blocks, share)
    for i, (ref, at) in enumerate(places):
        k_all[i * share : (i + 1) * share, :] = ref[at : at + share, :]
        v_all[i * share : (i + 1) * share, :] = ref[at + share : at + 2 * share, :]
    if own:
        k_all[len(places) * share :, :] = own[0][0]
        v_all[len(places) * share :, :] = own[1][0]
    return len(places) * share


def own_mask(at, resp):
    key_at = lax.broadcasted_iota(jnp.int32, (SLICE, resp), 0) + at
    return key_at <= lax.broadcasted_iota(jnp.int32, (SLICE, resp), 1)


def forward_kernel(heads, share, count, opening, *refs):
    refs, scratch = refs[:-6], refs[-6:]
    k_all, v_all, s0, s1, g0, g1 = scratch
    if opening:
        len_ref, q_ref, c_ref = refs[:3]
        blocks, own = refs[3 : 3 + count], refs[3 + count : 5 + count]
        out_ref, q_rows, c_rows = refs[5 + count :]
    else:
        q_rows, c_rows = refs[:2]
        blocks, own, out_ref = refs[2 : 2 + count], (), refs[-1]
    width, resp = q_rows.shape[1], q_rows.shape[0] // heads
    rate = math.log2(math.e) / math.sqrt(width)
    s_buf, g_buf = (s0, s1), (g0, g1)
    prompt = load_rows(blocks, own, k_all, v_all, share)
    keys = k_all.shape[0]
    if opening:
        live = lax.broadcasted_iota(jnp.int32, (resp, width), 0) < len_ref[0]

    for t in range(heads + 1):
        if t < heads:
            rows = slice(t * resp, (t + 1) * resp)
            if opening:
                lanes = slice(t * width, (t + 1) * width)
                q_rows[rows, :] = q_ref[0, :, lanes]
                c_rows[rows, :] = jnp.where(live, c_ref[0, :, lanes], jnp.zeros((), BF16))
            s_buf[t % 2][...] = dot_nt(k_all[...], q_rows[rows, :])
            g_buf[t % 2][...] = dot_nt(v_all[...], c_rows[rows, :])
        if t > 0:
            h = t - 1
            s_now, g_now = s_buf[h % 2], g_buf[h % 2]
            top = mass = mixed = None
            for at in range(0, keys, SLICE):
                s = s_now[at : at + SLICE, :]
                if at >= prompt:
                    s = jnp.where(own_mask(at - prompt, resp), s, -jnp.inf)
                part = fold_rows(s, jnp.maximum)
                top = part if top is None else jnp.maximum(top, part)
            top = jnp.max(top, axis=0, keepdims=True)
            level = top * rate
            for at in range(0, keys, SLICE):
                e = jnp.exp2(s_now[at : at + SLICE, :] * rate - level)
                if at >= prompt:
                    e = jnp.where(own_mask(at - prompt, resp), e, 0.0)
                part = fold_rows(e, jnp.add)
                mass = part if mass is None else mass + part
                part = fold_rows(e * g_now[at : at + SLICE, :], jnp.add)
                mixed = part if mixed is None else mixed + part
            out_ref[h : h + 1, :] = top
            out_ref[heads + h : heads + h + 1, :] = jnp.sum(mass, axis=0, keepdims=True)
            out_ref[2 * heads + h : 2 * heads + h + 1, :] = jnp.sum(mixed, axis=0, keepdims=True)
    paid = jnp.zeros((1, width), F32)
    for ref, at in pack_places(blocks, share):
        paid = paid + ref[at + 2 * share : at + 2 * share + PAD, :].astype(F32)[:1]
    out_ref[3 * heads :, :] = jnp.broadcast_to(jnp.max(paid), (heads, resp))


def backward_kernel(heads, share, owners, count, stats, after, more, last, *refs):
    refs, scratch = refs[:-7], refs[-7:]
    k_all, v_all, k_t, s_now, g_now, p_all, ds_all = scratch
    pay_ref, q_rows, c_rows = refs[:3]
    refs = refs[3:]
    stat_refs, refs = refs[:stats], refs[stats:]
    blocks, refs = refs[:count], refs[count:]
    own, refs = (refs[:2], refs[2:]) if last else ((), refs)
    prior, refs = (refs[0], refs[1:]) if more else (None, refs)
    refs = refs[after:]
    dq_ref, refs = refs[0], refs[1:]
    part_refs, own_out = refs[:count], refs[count:]
    width, resp = q_rows.shape[1], q_rows.shape[0] // heads
    scale = 1.0 / math.sqrt(width)
    rate = scale * math.log2(math.e)
    prompt = load_rows(blocks, own, k_all, v_all, share)
    keys = k_all.shape[0]

    peaks = [ref[:heads, :] for ref in stat_refs]
    peak = functools.reduce(jnp.maximum, peaks)
    mass, mixed, paid = 0.0, 0.0, 0.0
    for ref, local in zip(stat_refs, peaks):
        weight = jnp.exp2((local - peak) * rate)
        mass = mass + ref[heads : 2 * heads, :] * weight
        mixed = mixed + ref[2 * heads : 3 * heads, :] * weight
        paid = paid + ref[3 * heads :, :]
    level = peak * rate + jnp.log2(mass)
    delta = mixed / mass
    advantage = (pay_ref[0].astype(F32) - paid / owners)[:1, :width]

    for at in range(0, keys, share):
        k_t[:, at : at + share] = k_all[at : at + share, :].T
    half = heads // 2
    dk = dv = None
    for h in range(heads):
        rows = slice(h * resp, (h + 1) * resp)
        s_now[h % 2] = dot_nt(k_all[...], q_rows[rows, :])
        g_now[h % 2] = dot_nt(v_all[...], c_rows[rows, :])
        for at in range(0, keys, SLICE):
            here = slice(at, at + SLICE)
            p = jnp.exp2(s_now[h % 2, here, :] * rate - level[h : h + 1])
            if at >= prompt:
                p = jnp.where(own_mask(at - prompt, resp), p, 0.0)
            p_all[here, rows] = p.astype(BF16)
            ds_all[here, rows] = (p * (g_now[h % 2, here, :] - delta[h : h + 1])).astype(BF16)
        lanes = slice(h * width, (h + 1) * width)
        dq = dot_nn(k_t[...], ds_all[:, rows])
        if more:
            dq = dq + prior[lanes, :]
        if last:
            dq_ref[0, :, lanes] = dq.T * (advantage * scale)
        else:
            dq_ref[lanes, :] = dq
        if h % half == half - 1:
            block = slice((h + 1 - half) * resp, (h + 1) * resp)
            dk_part = dot_nn(ds_all[:, block], q_rows[block, :])
            dv_part = dot_nn(p_all[:, block], c_rows[block, :])
            dk = dk_part if dk is None else dk + dk_part
            dv = dv_part if dv is None else dv + dv_part
    dk, dv = dk * (advantage * scale), dv * advantage
    at = 0
    for ref in part_refs:
        for base in range(0, ref.shape[0], 2 * share):
            ref[base : base + share, :] = dk[at : at + share].astype(ref.dtype)
            ref[base + share : base + 2 * share, :] = dv[at : at + share].astype(ref.dtype)
            at += share
    if last:
        own_out[0][0] = dk[prompt:]
        own_out[1][0] = dv[prompt:]


def count_keys(blocks, share, own):
    return share * sum(b.shape[0] // (2 * share + PAD) for b in blocks) + (
        own[0].shape[1] if own else 0
    )


def forward_stats(heads, share, blocks, rows=(), opening=()):
    if opening:
        lengths, queries, grad_out, *own = opening
        resp, width = queries.shape[1], queries.shape[2] // heads
        operands = (lengths, queries, grad_out, *blocks, *own)
        specs = [SMEM_SPEC] + [VMEM_SPEC] * (len(operands) - 1)
    else:
        own = ()
        resp, width = rows[0].shape[0] // heads, rows[0].shape[1]
        operands = (*rows, *blocks)
        specs = [VMEM_SPEC] * len(operands)
    keys = count_keys(blocks, share, own)
    outs = [jax.ShapeDtypeStruct((4 * heads, resp), F32)]
    if opening:
        outs += [jax.ShapeDtypeStruct((heads * resp, width), BF16)] * 2
    return pl.pallas_call(
        functools.partial(forward_kernel, heads, share, len(blocks), bool(opening)),
        out_shape=tuple(outs),
        in_specs=specs,
        out_specs=(VMEM_SPEC,) * len(outs),
        scratch_shapes=[pltpu.VMEM((keys, width), BF16)] * 2 + [pltpu.VMEM((keys, resp), F32)] * 4,
        compiler_params=pltpu.CompilerParams(vmem_limit_bytes=24 * 1024 * 1024),
        cost_estimate=pl.CostEstimate(
            flops=12 * heads * resp * keys * width,
            bytes_accessed=1024 * 1024,
            transcendentals=heads * resp * keys,
        ),
        name="forward_stats",
    )(*operands)


def backward_grads(rewards, rows, stats, blocks, dtypes, owners, heads, share, own, prior, after):
    resp, width = rows[0].shape[0] // heads, rows[0].shape[1]
    last, more = bool(own), prior is not None
    keys = count_keys(blocks, share, own)
    dq_shape = (1, resp, heads * width) if last else (heads * width, resp)
    outs = [jax.ShapeDtypeStruct(dq_shape, F32)]
    for block, dtype in zip(blocks, dtypes):
        packs = block.shape[0] // (2 * share + PAD)
        outs.append(jax.ShapeDtypeStruct((packs * 2 * share, width), dtype))
    outs += [jax.ShapeDtypeStruct((1, resp, width), F32)] * len(own)
    operands = (*rows, *stats, *blocks, *own, *((prior,) if more else ()))
    return pl.pallas_call(
        functools.partial(
            backward_kernel, heads, share, owners, len(blocks), len(stats), len(after), more, last
        ),
        out_shape=tuple(outs),
        in_specs=[SMEM_SPEC] + [VMEM_SPEC] * len(operands) + [ANY_SPEC] * len(after),
        out_specs=(VMEM_SPEC,) * len(outs),
        scratch_shapes=[pltpu.VMEM((keys, width), BF16)] * 2
        + [pltpu.VMEM((width, keys), BF16)]
        + [pltpu.VMEM((2, keys, resp), F32)] * 2
        + [pltpu.VMEM((keys, heads * resp), BF16)] * 2,
        compiler_params=pltpu.CompilerParams(vmem_limit_bytes=24 * 1024 * 1024),
        cost_estimate=pl.CostEstimate(
            flops=30 * heads * resp * keys * width,
            bytes_accessed=2 * 1024 * 1024,
            transcendentals=heads * resp * keys,
        ),
        name="backward_grads",
    )(rewards, *operands, *after)


def send(block, plane, step):
    pairs = [
        (y * RING + z, (y + plane) % 2 * RING + (z + step) % RING)
        for y in range(2)
        for z in range(RING)
    ]
    return lax.ppermute(block, "sample", pairs)


def shards(queries, resp_keys, resp_values, prompt_keys, prompt_values, grad_out, lengths, rewards):
    share, width = prompt_keys.shape
    heads = queries.shape[2] // width
    owners = lax.axis_size("sample")
    reward_rows = jnp.broadcast_to(rewards.astype(BF16)[:, None], (PAD, width))
    packed = jnp.concatenate([prompt_keys, prompt_values, reward_rows], axis=0)

    swapped = send(packed, 1, 0)
    pairs = {0: jnp.concatenate([packed, swapped], axis=0)}
    for step in (1, 2, 3, 4):
        pairs[step] = send(pairs[step - 1], 0, 1)
        if step < 4:
            pairs[RING - step] = send(pairs[(RING - step + 1) % RING], 0, -1)

    own = (resp_keys, resp_values)
    first, *rows = forward_stats(
        heads, share, [packed], opening=(lengths, queries, grad_out, *own)
    )
    stats = [first]
    for blocks in ([swapped], [pairs[1], pairs[7]], [pairs[2], pairs[6]], [pairs[3], pairs[5]], [pairs[4]]):
        stats += forward_stats(heads, share, blocks, rows)

    back = functools.partial(
        backward_grads, rewards, rows, stats, owners=owners, heads=heads, share=share
    )

    def add(received, part):
        return (received.astype(F32) + part).astype(BF16)

    dq, down = back([pairs[4]], [BF16], own=(), prior=None, after=())
    dq, part, up = back([pairs[3], pairs[5]], [F32, BF16], own=(), prior=dq, after=())
    down = add(send(down, 0, -1), part)
    for step in (2, 1):
        dq, part_down, part_up = back(
            [pairs[step], pairs[RING - step]], [F32, F32], own=(), prior=dq, after=(down, up)
        )
        down = add(send(down, 0, -1), part_down)
        up = add(send(up, 0, 1), part_up)
    grad_queries, mine, grad_resp_keys, grad_resp_values = back(
        [pairs[0]], [F32], own=own, prior=dq, after=(down, up)
    )
    mine = mine + send(down, 0, -1).astype(F32) + send(up, 0, 1).astype(F32)
    total = mine[: 2 * share] + send(mine[2 * share :].astype(BF16), 1, 0).astype(F32)
    return grad_queries, grad_resp_keys, grad_resp_values, total[:share], total[share:]


def solution(mesh):
    whole = P(("problem", "sample"), None, None)
    rows = P(("problem", "sample"), None)
    one = P(("problem", "sample"))
    return jax.shard_map(
        shards,
        mesh=mesh,
        in_specs=(whole, whole, whole, rows, rows, whole, one, one),
        out_specs=(whole, whole, whole, rows, rows),
        check_vma=False,
    )
```

```python
import functools
import math

import jax
import jax.numpy as jnp
from jax import lax
from jax.experimental import pallas as pl
from jax.experimental.pallas import tpu as pltpu
from jax.sharding import PartitionSpec as P

F32 = jnp.float32
BF16 = jnp.bfloat16
PAD = 16
RING = 8
SLICE = 64
SCOPED = 20 * 1024 * 1024

VMEM_SPEC = pl.BlockSpec(memory_space=pltpu.VMEM)
SMEM_SPEC = pl.BlockSpec(memory_space=pltpu.SMEM)
ANY_SPEC = pl.BlockSpec(memory_space=pl.ANY)


def dot_nn(left, right):
    return lax.dot_general(left, right, (((1,), (0,)), ((), ())), preferred_element_type=F32)


def dot_nt(left, right):
    return lax.dot_general(left, right, (((1,), (1,)), ((), ())), preferred_element_type=F32)


def fold_rows(values, combine):
    parts = [values[i : i + 8] for i in range(0, values.shape[0], 8)]
    while len(parts) > 1:
        parts = [
            combine(parts[i], parts[i + 1]) if i + 1 < len(parts) else parts[i]
            for i in range(0, len(parts), 2)
        ]
    return parts[0]


def pack_places(blocks, share):
    size = 2 * share + PAD
    return [(ref, at) for ref in blocks for at in range(0, ref.shape[0], size)]


def load_rows(blocks, own, k_all, v_all, share):
    places = pack_places(blocks, share)
    for i, (ref, at) in enumerate(places):
        k_all[i * share : (i + 1) * share, :] = ref[at : at + share, :]
        v_all[i * share : (i + 1) * share, :] = ref[at + share : at + 2 * share, :]
    if own:
        k_all[len(places) * share :, :] = own[0][0]
        v_all[len(places) * share :, :] = own[1][0]
    return len(places) * share


def own_mask(at, resp):
    key_at = lax.broadcasted_iota(jnp.int32, (SLICE, resp), 0) + at
    return key_at <= lax.broadcasted_iota(jnp.int32, (SLICE, resp), 1)


def forward_kernel(heads, share, count, opening, *refs):
    refs, scratch = refs[:-4], refs[-4:]
    k_all, v_all, s0, s1 = scratch
    if opening:
        len_ref, q_ref, c_ref = refs[:3]
        blocks, own = refs[3 : 3 + count], refs[3 + count : 5 + count]
        out_ref, e_all, g_all, q_rows, c_rows, copy_ref = refs[5 + count :]
        copy_ref[...] = blocks[0][...]
    else:
        q_rows, c_rows = refs[:2]
        blocks, own = refs[2 : 2 + count], ()
        out_ref, e_all, g_all = refs[2 + count :]
    width, resp = q_rows.shape[1], q_rows.shape[0] // heads
    rate = math.log2(math.e) / math.sqrt(width)
    s_buf = (s0, s1)
    prompt = load_rows(blocks, own, k_all, v_all, share)
    keys = k_all.shape[0]
    if opening:
        live = lax.broadcasted_iota(jnp.int32, (resp, width), 0) < len_ref[0]

    for t in range(heads + 1):
        if t < heads:
            rows = slice(t * resp, (t + 1) * resp)
            if opening:
                lanes = slice(t * width, (t + 1) * width)
                q_rows[rows, :] = q_ref[0, :, lanes]
                c_rows[rows, :] = jnp.where(live, c_ref[0, :, lanes], jnp.zeros((), BF16))
            s_buf[t % 2][...] = dot_nt(k_all[...], q_rows[rows, :])
            g_all[:, rows] = dot_nt(v_all[...], c_rows[rows, :])
        if t > 0:
            h = t - 1
            s_now, cols = s_buf[h % 2], slice(h * resp, (h + 1) * resp)
            top = mass = mixed = None
            for at in range(0, keys, SLICE):
                s = s_now[at : at + SLICE, :]
                if at >= prompt:
                    s = jnp.where(own_mask(at - prompt, resp), s, -jnp.inf)
                part = fold_rows(s, jnp.maximum)
                top = part if top is None else jnp.maximum(top, part)
            top = jnp.max(top, axis=0, keepdims=True)
            level = top * rate
            for at in range(0, keys, SLICE):
                here = slice(at, at + SLICE)
                e = jnp.exp2(s_now[here, :] * rate - level)
                if at >= prompt:
                    e = jnp.where(own_mask(at - prompt, resp), e, 0.0)
                e_all[here, cols] = e.astype(BF16)
                part = fold_rows(e, jnp.add)
                mass = part if mass is None else mass + part
                part = fold_rows(e * g_all[here, cols], jnp.add)
                mixed = part if mixed is None else mixed + part
            out_ref[h : h + 1, :] = top
            out_ref[heads + h : heads + h + 1, :] = jnp.sum(mass, axis=0, keepdims=True)
            out_ref[2 * heads + h : 2 * heads + h + 1, :] = jnp.sum(mixed, axis=0, keepdims=True)
    paid = jnp.zeros((1, width), F32)
    for ref, at in pack_places(blocks, share):
        paid = paid + ref[at + 2 * share : at + 2 * share + PAD, :].astype(F32)[:1]
    out_ref[3 * heads :, :] = jnp.broadcast_to(jnp.max(paid), (heads, resp))


def backward_kernel(heads, share, owners, count, stats, spans, after, more, last, *refs):
    refs, (k_t, p_all, ds_all) = refs[:-3], refs[-3:]
    pay_ref, q_rows, c_rows = refs[:3]
    refs = refs[3:]
    stat_refs, refs = refs[:stats], refs[stats:]
    e_refs, g_refs, refs = refs[: len(spans)], refs[len(spans) : 2 * len(spans)], refs[2 * len(spans) :]
    blocks, refs = refs[:count], refs[count:]
    prior, refs = (refs[0], refs[1:]) if more else (None, refs)
    dq_ref, *out_refs = refs[after:]
    width, resp = q_rows.shape[1], q_rows.shape[0] // heads
    scale = 1.0 / math.sqrt(width)
    rate = scale * math.log2(math.e)

    peaks = [ref[:heads, :] for ref in stat_refs]
    peak = functools.reduce(jnp.maximum, peaks)
    weights = [jnp.exp2((local - peak) * rate) for local in peaks]
    mass, mixed, paid = 0.0, 0.0, 0.0
    for ref, weight in zip(stat_refs, weights):
        mass = mass + ref[heads : 2 * heads, :] * weight
        mixed = mixed + ref[2 * heads : 3 * heads, :] * weight
        paid = paid + ref[3 * heads :, :]
    delta = mixed / mass
    factors = [weights[group] / mass for group, _, _ in spans]
    advantage = (pay_ref[0].astype(F32) - paid / owners)[:1, :width]

    if last:
        k_t[...] = blocks[0][0].T
    else:
        for i, (ref, at) in enumerate(pack_places(blocks, share)):
            k_t[:, i * share : (i + 1) * share] = ref[at : at + share, :].T
    half = heads // 2
    dk = dv = None
    for h in range(heads):
        cols = slice(h * resp, (h + 1) * resp)
        to = 0
        for (_, first, size), e_ref, g_ref, factor in zip(spans, e_refs, g_refs, factors):
            for at in range(first, first + size, SLICE):
                p = e_ref[at : at + SLICE, cols].astype(F32) * factor[h : h + 1]
                ds = p * (g_ref[at : at + SLICE, cols] - delta[h : h + 1])
                p_all[to : to + SLICE, cols] = p.astype(BF16)
                ds_all[to : to + SLICE, cols] = ds.astype(BF16)
                to += SLICE
        lanes = slice(h * width, (h + 1) * width)
        dq = dot_nn(k_t[...], ds_all[:, cols])
        if more:
            dq = dq + prior[lanes, :]
        if last:
            dq_ref[0, :, lanes] = dq.T * (advantage * scale)
        else:
            dq_ref[lanes, :] = dq
        if h % half == half - 1:
            block = slice((h + 1 - half) * resp, (h + 1) * resp)
            dk_part = dot_nn(ds_all[:, block], q_rows[block, :])
            dv_part = dot_nn(p_all[:, block], c_rows[block, :])
            dk = dk_part if dk is None else dk + dk_part
            dv = dv_part if dv is None else dv + dv_part
    dk, dv = dk * (advantage * scale), dv * advantage
    if last:
        out_refs[0][0] = dk
        out_refs[1][0] = dv
        return
    at = 0
    for ref in out_refs:
        for base in range(0, ref.shape[0], 2 * share):
            ref[base : base + share, :] = dk[at : at + share].astype(ref.dtype)
            ref[base + share : base + 2 * share, :] = dv[at : at + share].astype(ref.dtype)
            at += share


def count_keys(blocks, share, own):
    return share * sum(b.shape[0] // (2 * share + PAD) for b in blocks) + (
        own[0].shape[1] if own else 0
    )


def forward_stats(heads, share, blocks, rows=(), opening=()):
    if opening:
        lengths, queries, grad_out, *own = opening
        resp, width = queries.shape[1], queries.shape[2] // heads
        operands = (lengths, queries, grad_out, *blocks, *own)
        specs = [SMEM_SPEC] + [VMEM_SPEC] * (len(operands) - 1)
    else:
        own = ()
        resp, width = rows[0].shape[0] // heads, rows[0].shape[1]
        operands = (*rows, *blocks)
        specs = [VMEM_SPEC] * len(operands)
    keys = count_keys(blocks, share, own)
    outs = [
        jax.ShapeDtypeStruct((4 * heads, resp), F32),
        jax.ShapeDtypeStruct((keys, heads * resp), BF16),
        jax.ShapeDtypeStruct((keys, heads * resp), F32),
    ]
    if opening:
        outs += [jax.ShapeDtypeStruct((heads * resp, width), BF16)] * 2
        outs += [jax.ShapeDtypeStruct(blocks[0].shape, BF16)]
    return pl.pallas_call(
        functools.partial(forward_kernel, heads, share, len(blocks), bool(opening)),
        out_shape=tuple(outs),
        in_specs=specs,
        out_specs=(VMEM_SPEC,) * len(outs),
        scratch_shapes=[pltpu.VMEM((keys, width), BF16)] * 2 + [pltpu.VMEM((keys, resp), F32)] * 2,
        compiler_params=pltpu.CompilerParams(vmem_limit_bytes=SCOPED),
        cost_estimate=pl.CostEstimate(
            flops=12 * heads * resp * keys * width,
            bytes_accessed=1024 * 1024,
            transcendentals=heads * resp * keys,
        ),
        name="forward_stats",
    )(*operands)


def backward_grads(
    rewards, rows, stats, kept, parts, blocks, outs, owners, heads, share, prior, after, last=False
):
    resp, width = rows[0].shape[0] // heads, rows[0].shape[1]
    more = prior is not None
    keys = sum(size for _, _, size in parts)
    dq_shape = (1, resp, heads * width) if last else (heads * width, resp)
    outs = [jax.ShapeDtypeStruct(dq_shape, F32), *outs]
    operands = (
        *rows, *stats, *(kept[g][0] for g, _, _ in parts), *(kept[g][1] for g, _, _ in parts),
        *blocks, *((prior,) if more else ()),
    )
    return pl.pallas_call(
        functools.partial(
            backward_kernel, heads, share, owners, len(blocks), len(stats), parts, len(after),
            more, last,
        ),
        out_shape=tuple(outs),
        in_specs=[SMEM_SPEC] + [VMEM_SPEC] * len(operands) + [ANY_SPEC] * len(after),
        out_specs=(VMEM_SPEC,) * len(outs),
        scratch_shapes=[pltpu.VMEM((width, keys), BF16)]
        + [pltpu.VMEM((keys, heads * resp), BF16)] * 2,
        compiler_params=pltpu.CompilerParams(vmem_limit_bytes=SCOPED),
        cost_estimate=pl.CostEstimate(
            flops=20 * heads * resp * keys * width,
            bytes_accessed=2 * 1024 * 1024,
            transcendentals=0,
        ),
        name="backward_grads",
    )(rewards, *operands, *after)


def send(block, plane, step):
    pairs = [
        (y * RING + z, (y + plane) % 2 * RING + (z + step) % RING)
        for y in range(2)
        for z in range(RING)
    ]
    return lax.ppermute(block, "sample", pairs)


def shards(queries, resp_keys, resp_values, prompt_keys, prompt_values, grad_out, lengths, rewards):
    share, width = prompt_keys.shape
    resp = queries.shape[1]
    heads = queries.shape[2] // width
    owners = lax.axis_size("sample")
    reward_rows = jnp.broadcast_to(rewards.astype(BF16)[:, None], (PAD, width))
    packed = jnp.concatenate([prompt_keys, prompt_values, reward_rows], axis=0)

    swapped = send(packed, 1, 0)
    first, *keep, q_rows, c_rows, packed = forward_stats(
        heads, share, [packed], opening=(lengths, queries, grad_out, resp_keys, resp_values)
    )
    rows, stats, kept = (q_rows, c_rows), [first], [keep]
    pairs = {0: jnp.concatenate([packed, swapped], axis=0)}
    for step in (1, 2, 3, 4):
        pairs[step] = send(pairs[step - 1], 0, 1)
        if step < 4:
            pairs[RING - step] = send(pairs[(RING - step + 1) % RING], 0, -1)
    for blocks in ([swapped], [pairs[1], pairs[7]], [pairs[2], pairs[6]], [pairs[3], pairs[5]], [pairs[4]]):
        stat, *keep = forward_stats(heads, share, blocks, rows)
        stats.append(stat)
        kept.append(keep)

    back = functools.partial(
        backward_grads, rewards, rows, stats, kept, owners=owners, heads=heads, share=share
    )
    ready = jax.ShapeDtypeStruct((4 * share, width), BF16)
    wide = jax.ShapeDtypeStruct((4 * share, width), F32)
    grads = jax.ShapeDtypeStruct((1, resp, width), F32)

    def add(received, part):
        return (received.astype(F32) + part).astype(BF16)

    dq, down = back(((5, 0, 2 * share),), [pairs[4]], [ready], prior=None, after=())
    dq, part, up = back(
        ((4, 0, 4 * share),), [pairs[3], pairs[5]], [wide, ready], prior=dq, after=()
    )
    down = add(send(down, 0, -1), part)
    for step in (2, 1):
        dq, part_down, part_up = back(
            ((step + 1, 0, 4 * share),), [pairs[step], pairs[RING - step]], [wide, wide],
            prior=dq, after=(down, up),
        )
        down = add(send(down, 0, -1), part_down)
        up = add(send(up, 0, 1), part_up)
    dq, mine = back(
        ((0, 0, share), (1, 0, share)), [packed, swapped], [wide], prior=dq, after=(down, up)
    )
    mine = mine + send(down, 0, -1).astype(F32) + send(up, 0, 1).astype(F32)
    partner = mine[2 * share :].astype(BF16)
    grad_queries, grad_resp_keys, grad_resp_values = back(
        ((0, share, resp),), [resp_keys], [grads, grads], prior=dq, after=(partner,), last=True
    )
    theirs = send(partner, 1, 0).astype(F32)
    return (
        grad_queries, grad_resp_keys, grad_resp_values,
        mine[:share] + theirs[:share], mine[share : 2 * share] + theirs[share:],
    )


def solution(mesh):
    whole = P(("problem", "sample"), None, None)
    rows = P(("problem", "sample"), None)
    one = P(("problem", "sample"))
    return jax.shard_map(
        shards,
        mesh=mesh,
        in_specs=(whole, whole, whole, rows, rows, whole, one, one),
        out_specs=(whole, whole, whole, rows, rows),
        check_vma=False,
    )
```

```python
import functools
import math

import jax
import jax.numpy as jnp
from jax import lax
from jax.experimental import pallas as pl
from jax.experimental.pallas import tpu as pltpu
from jax.sharding import PartitionSpec as P

F32 = jnp.float32
BF16 = jnp.bfloat16
PAD = 16
RING = 8
SLICE = 64
SCOPED = 20 * 1024 * 1024

VMEM_SPEC = pl.BlockSpec(memory_space=pltpu.VMEM)
SMEM_SPEC = pl.BlockSpec(memory_space=pltpu.SMEM)
ANY_SPEC = pl.BlockSpec(memory_space=pl.ANY)


def dot_nn(left, right):
    return lax.dot_general(left, right, (((1,), (0,)), ((), ())), preferred_element_type=F32)


def dot_nt(left, right):
    return lax.dot_general(left, right, (((1,), (1,)), ((), ())), preferred_element_type=F32)


def fold_rows(values, combine):
    parts = [values[i : i + 8] for i in range(0, values.shape[0], 8)]
    while len(parts) > 1:
        parts = [
            combine(parts[i], parts[i + 1]) if i + 1 < len(parts) else parts[i]
            for i in range(0, len(parts), 2)
        ]
    return parts[0]


def pack_places(blocks, picks, share):
    size = 2 * share + PAD
    return [
        (ref, (first + i) * size)
        for ref, (first, count) in zip(blocks, picks)
        for i in range(count)
    ]


def own_mask(at, resp):
    key_at = lax.broadcasted_iota(jnp.int32, (SLICE, resp), 0) + at
    return key_at <= lax.broadcasted_iota(jnp.int32, (SLICE, resp), 1)


def forward_kernel(heads, share, picks, opening, *refs):
    refs, scratch = refs[:-4], refs[-4:]
    k_all, v_all, s0, s1 = scratch
    count = len(picks)
    if opening:
        len_ref, wide_ref, own_ref = refs[:3]
        blocks = refs[3 : 3 + count]
        out_ref, e_all, g_all, q_rows, c_rows = refs[3 + count :]
    else:
        q_rows, c_rows = refs[:2]
        blocks = refs[2 : 2 + count]
        out_ref, e_all, g_all = refs[2 + count :]
    width, resp = q_rows.shape[1], q_rows.shape[0] // heads
    rate = math.log2(math.e) / math.sqrt(width)
    s_buf = (s0, s1)
    keys = k_all.shape[0]
    places = pack_places(blocks, picks, share)
    prompt = len(places) * share
    for i, (ref, at) in enumerate(places):
        k_all[i * share : (i + 1) * share, :] = ref[at : at + share, :]
        v_all[i * share : (i + 1) * share, :] = ref[at + share : at + 2 * share, :]
    if opening:
        k_all[prompt:, :] = own_ref[0]
        v_all[prompt:, :] = own_ref[1]
        live = lax.broadcasted_iota(jnp.int32, (resp, width), 0) < len_ref[0]

    for t in range(heads + 1):
        if t < heads:
            rows = slice(t * resp, (t + 1) * resp)
            if opening:
                lanes = slice(t * width, (t + 1) * width)
                q_rows[rows, :] = wide_ref[0, :, lanes]
                c_rows[rows, :] = jnp.where(live, wide_ref[1, :, lanes], jnp.zeros((), BF16))
            s_buf[t % 2][...] = dot_nt(k_all[...], q_rows[rows, :])
            g_all[:, rows] = dot_nt(v_all[...], c_rows[rows, :])
        if t > 0:
            h = t - 1
            s_now, cols = s_buf[h % 2], slice(h * resp, (h + 1) * resp)
            top = mass = mixed = None
            for at in range(0, keys, SLICE):
                s = s_now[at : at + SLICE, :]
                if at >= prompt:
                    s = jnp.where(own_mask(at - prompt, resp), s, -jnp.inf)
                part = fold_rows(s, jnp.maximum)
                top = part if top is None else jnp.maximum(top, part)
            top = jnp.max(top, axis=0, keepdims=True)
            level = top * rate
            for at in range(0, keys, SLICE):
                here = slice(at, at + SLICE)
                e = jnp.exp2(s_now[here, :] * rate - level)
                if at >= prompt:
                    e = jnp.where(own_mask(at - prompt, resp), e, 0.0)
                e_all[here, cols] = e.astype(BF16)
                part = fold_rows(e, jnp.add)
                mass = part if mass is None else mass + part
                part = fold_rows(e * g_all[here, cols], jnp.add)
                mixed = part if mixed is None else mixed + part
            out_ref[h : h + 1, :] = top
            out_ref[heads + h : heads + h + 1, :] = jnp.sum(mass, axis=0, keepdims=True)
            out_ref[2 * heads + h : 2 * heads + h + 1, :] = jnp.sum(mixed, axis=0, keepdims=True)
    paid = jnp.zeros((1, width), F32)
    for ref, at in places:
        paid = paid + ref[at + 2 * share : at + 2 * share + PAD, :].astype(F32)[:1]
    out_ref[3 * heads :, :] = jnp.broadcast_to(jnp.max(paid), (heads, resp))


def backward_kernel(heads, share, owners, picks, stats, spans, after, more, last, *refs):
    refs, (k_t, p_all, ds_all) = refs[:-3], refs[-3:]
    pay_ref, q_rows, c_rows = refs[:3]
    refs = refs[3:]
    stat_refs, refs = refs[:stats], refs[stats:]
    e_refs, g_refs, refs = refs[: len(spans)], refs[len(spans) : 2 * len(spans)], refs[2 * len(spans) :]
    blocks, refs = refs[: len(picks)], refs[len(picks) :]
    own_ref, refs = (refs[0], refs[1:]) if last else (None, refs)
    prior, refs = (refs[0], refs[1:]) if more else (None, refs)
    dq_ref, *out_refs = refs[after:]
    width, resp = q_rows.shape[1], q_rows.shape[0] // heads
    scale = 1.0 / math.sqrt(width)
    rate = scale * math.log2(math.e)

    peaks = [ref[:heads, :] for ref in stat_refs]
    peak = functools.reduce(jnp.maximum, peaks)
    weights = [jnp.exp2((local - peak) * rate) for local in peaks]
    mass, mixed, paid = 0.0, 0.0, 0.0
    for ref, weight in zip(stat_refs, weights):
        mass = mass + ref[heads : 2 * heads, :] * weight
        mixed = mixed + ref[2 * heads : 3 * heads, :] * weight
        paid = paid + ref[3 * heads :, :]
    delta = mixed / mass
    factors = [weights[group] / mass for group, _, _ in spans]
    advantage = (pay_ref[0].astype(F32) - paid / owners)[:1, :width]

    places = pack_places(blocks, picks, share)
    for i, (ref, at) in enumerate(places):
        k_t[:, i * share : (i + 1) * share] = ref[at : at + share, :].T
    prompt = len(places) * share
    if last:
        k_t[:, prompt:] = own_ref[0].T
    half = heads // 2
    dk = dv = None
    for h in range(heads):
        cols = slice(h * resp, (h + 1) * resp)
        to = 0
        for (_, first, size), e_ref, g_ref, factor in zip(spans, e_refs, g_refs, factors):
            for at in range(first, first + size, SLICE):
                p = e_ref[at : at + SLICE, cols].astype(F32) * factor[h : h + 1]
                ds = p * (g_ref[at : at + SLICE, cols] - delta[h : h + 1])
                p_all[to : to + SLICE, cols] = p.astype(BF16)
                ds_all[to : to + SLICE, cols] = ds.astype(BF16)
                to += SLICE
        lanes = slice(h * width, (h + 1) * width)
        dq = dot_nn(k_t[...], ds_all[:, cols])
        if more:
            dq = dq + prior[lanes, :]
        if last:
            dq_ref[0, :, lanes] = dq.T * (advantage * scale)
        else:
            dq_ref[lanes, :] = dq
        if h % half == half - 1:
            block = slice((h + 1 - half) * resp, (h + 1) * resp)
            dk_part = dot_nn(ds_all[:, block], q_rows[block, :])
            dv_part = dot_nn(p_all[:, block], c_rows[block, :])
            dk = dk_part if dk is None else dk + dk_part
            dv = dv_part if dv is None else dv + dv_part
    dk, dv = dk * (advantage * scale), dv * advantage
    if last:
        *out_refs, own_keys, own_values = out_refs
        own_keys[0] = dk[prompt:]
        own_values[0] = dv[prompt:]
    at = 0
    for ref in out_refs:
        for base in range(0, ref.shape[0], 2 * share):
            ref[base : base + share, :] = dk[at : at + share].astype(ref.dtype)
            ref[base + share : base + 2 * share, :] = dv[at : at + share].astype(ref.dtype)
            at += share


def forward_stats(heads, share, blocks, rows=(), opening=()):
    if opening:
        resp, width = opening[1].shape[1], blocks[0].shape[1]
        operands = (*opening, *blocks)
        specs = [SMEM_SPEC] + [VMEM_SPEC] * (len(operands) - 1)
        picks = ((0, 1),)
    else:
        resp, width = rows[0].shape[0] // heads, rows[0].shape[1]
        operands = (*rows, *blocks)
        specs = [VMEM_SPEC] * len(operands)
        picks = tuple((0, block.shape[0] // (2 * share + PAD)) for block in blocks)
    keys = share * sum(count for _, count in picks) + (resp if opening else 0)
    outs = [
        jax.ShapeDtypeStruct((4 * heads, resp), F32),
        jax.ShapeDtypeStruct((keys, heads * resp), BF16),
        jax.ShapeDtypeStruct((keys, heads * resp), F32),
    ]
    if opening:
        outs += [jax.ShapeDtypeStruct((heads * resp, width), BF16)] * 2
    return pl.pallas_call(
        functools.partial(forward_kernel, heads, share, picks, bool(opening)),
        out_shape=tuple(outs),
        in_specs=specs,
        out_specs=(VMEM_SPEC,) * len(outs),
        scratch_shapes=[pltpu.VMEM((keys, width), BF16)] * 2 + [pltpu.VMEM((keys, resp), F32)] * 2,
        compiler_params=pltpu.CompilerParams(vmem_limit_bytes=SCOPED),
        cost_estimate=pl.CostEstimate(
            flops=12 * heads * resp * keys * width,
            bytes_accessed=1024 * 1024,
            transcendentals=heads * resp * keys,
        ),
        name="forward_stats",
    )(*operands)


def backward_grads(
    rewards, rows, stats, kept, parts, blocks, outs, owners, heads, share, prior, after, last=()
):
    blocks, picks = [block for block, _, _ in blocks], tuple(pick for _, *pick in blocks)
    resp, width = rows[0].shape[0] // heads, rows[0].shape[1]
    more = prior is not None
    keys = sum(size for _, _, size in parts)
    dq_shape = (1, resp, heads * width) if last else (heads * width, resp)
    outs = [jax.ShapeDtypeStruct(dq_shape, F32), *outs]
    operands = (
        *rows, *stats, *(kept[g][0] for g, _, _ in parts), *(kept[g][1] for g, _, _ in parts),
        *blocks, *last, *((prior,) if more else ()),
    )
    return pl.pallas_call(
        functools.partial(
            backward_kernel, heads, share, owners, picks, len(stats), parts, len(after),
            more, bool(last),
        ),
        out_shape=tuple(outs),
        in_specs=[SMEM_SPEC] + [VMEM_SPEC] * len(operands) + [ANY_SPEC] * len(after),
        out_specs=(VMEM_SPEC,) * len(outs),
        scratch_shapes=[pltpu.VMEM((width, keys), BF16)]
        + [pltpu.VMEM((keys, heads * resp), BF16)] * 2,
        compiler_params=pltpu.CompilerParams(vmem_limit_bytes=SCOPED),
        cost_estimate=pl.CostEstimate(
            flops=20 * heads * resp * keys * width,
            bytes_accessed=2 * 1024 * 1024,
            transcendentals=0,
        ),
        name="backward_grads",
    )(rewards, *operands, *after)


def tie(block, after):
    return pl.pallas_call(
        lambda block_ref, after_ref, out_ref: None,
        out_shape=jax.ShapeDtypeStruct(block.shape, block.dtype),
        in_specs=[ANY_SPEC] * 2,
        out_specs=ANY_SPEC,
        input_output_aliases={0: 0},
        compiler_params=pltpu.CompilerParams(vmem_limit_bytes=1024 * 1024),
        cost_estimate=pl.CostEstimate(flops=0, bytes_accessed=0, transcendentals=0),
        name="tie",
    )(block, after)


def across(block):
    pairs = [(i, (i + RING) % (2 * RING)) for i in range(2 * RING)]
    return lax.ppermute(block, "sample", pairs)


def along(block, side):
    pairs = []
    for y in range(2):
        for z in range(RING):
            other = (z + (1 if z % 2 == side else -1)) % RING
            pairs.append((y * RING + z, y * RING + other))
    return lax.ppermute(block, "sample", pairs)


def shards(queries, resp_keys, resp_values, prompt_keys, prompt_values, grad_out, lengths, rewards):
    share, width = prompt_keys.shape
    resp = queries.shape[1]
    heads = queries.shape[2] // width
    owners = lax.axis_size("sample")
    size = 2 * share
    reward_rows = jnp.broadcast_to(rewards.astype(BF16)[:, None], (PAD, width))
    packed = jnp.concatenate([prompt_keys, prompt_values, reward_rows], axis=0)
    own_rows = jnp.concatenate([resp_keys, resp_values], axis=0)
    wide_rows = jnp.concatenate([queries, grad_out], axis=0)

    first, *keep, q_rows, c_rows = forward_stats(
        heads, share, [packed], opening=(lengths, wide_rows, own_rows)
    )
    rows, stats, kept = (q_rows, c_rows), [first], [keep]

    def forward(*blocks):
        stat, *keep = forward_stats(heads, share, blocks, rows)
        stats.append(stat)
        kept.append(keep)

    def join(*blocks):
        return jnp.concatenate(blocks, axis=0)

    l1, r1 = along(packed, 0), along(packed, 1)
    l2, r2 = along(r1, 0), along(l1, 1)
    other1 = across(join(tie(packed, stats[-1]), l1, r1))
    forward(l1, r1)
    l2, r2 = tie(l2, stats[-1]), tie(r2, stats[-1])
    l3, r3 = along(r2, 0), along(l2, 1)
    other2 = across(join(l2, r2))
    forward(l2, r2)
    l3, r3 = tie(l3, stats[-1]), tie(r3, stats[-1])
    l4 = along(r3, 0)
    other3 = across(join(l3, r3))
    forward(other1, l3, r3)
    l4 = tie(l4, stats[-1])
    other4 = across(l4)
    forward(other2, l4)
    forward(other3)
    forward(other4)

    back = functools.partial(
        backward_grads, rewards, rows, stats, kept, owners=owners, heads=heads, share=share
    )
    ready = jax.ShapeDtypeStruct((size, width), BF16)
    both_ready = jax.ShapeDtypeStruct((2 * size, width), BF16)
    wide = jax.ShapeDtypeStruct((size, width), F32)
    grads = jax.ShapeDtypeStruct((1, resp, width), F32)

    def add(part, *received):
        return sum((r.astype(F32) for r in received), part).astype(BF16)

    dq, part = back(((6, 0, share),), [(other4, 0, 1)], [ready], prior=None, after=())
    given = across(part)
    dq, part, part_left = back(
        ((5, 0, size), (4, size, share)), [(other3, 0, 2), (l4, 0, 1)], [both_ready, wide],
        prior=dq, after=(),
    )
    far = add(part_left, given)
    given = across(part)
    dq, part, part_left, part_right = back(
        ((4, 0, size), (3, 3 * share, size)), [(other2, 0, 2), (l3, 0, 1), (r3, 0, 1)],
        [both_ready, wide, wide], prior=dq, after=(far,),
    )
    near = add(part_left, given[:size])
    far = add(part_right, given[size:], along(far, 0))
    given = across(part)
    dq, part, part_left, part_right = back(
        ((3, share, size), (2, 0, size)), [(other1, 1, 2), (l2, 0, 1), (r2, 0, 1)],
        [both_ready, wide, wide], prior=dq, after=(far, near),
    )
    near = add(part_right, given[size:], along(near, 0))
    far = add(part_left, given[:size], along(far, 1))
    given = across(part)
    dq, part, part_left, part_right = back(
        ((3, 0, share), (1, 0, size)), [(other1, 0, 1), (l1, 0, 1), (r1, 0, 1)],
        [ready, wide, wide], prior=dq, after=(far, near),
    )
    near = add(part_left, given[:size], along(near, 1))
    far = add(part_right, given[size:], along(far, 0))
    given = across(part)
    grad_queries, mine, grad_resp_keys, grad_resp_values = back(
        ((0, 0, share + resp),), [(packed, 0, 1)], [wide, grads, grads], prior=dq,
        after=(far, near), last=(own_rows,),
    )
    near, far = along(near, 0), along(far, 1)
    total = [
        mine[at : at + share] + sum(r[at : at + share].astype(F32) for r in (given, near, far))
        for at in (0, share)
    ]
    return grad_queries, grad_resp_keys, grad_resp_values, *total


def solution(mesh):
    whole = P(("problem", "sample"), None, None)
    rows = P(("problem", "sample"), None)
    one = P(("problem", "sample"))
    return jax.shard_map(
        shards,
        mesh=mesh,
        in_specs=(whole, whole, whole, rows, rows, whole, one, one),
        out_specs=(whole, whole, whole, rows, rows),
        check_vma=False,
    )
```

```python
import functools
import math

import jax
import jax.numpy as jnp
from jax import lax
from jax.experimental import pallas as pl
from jax.experimental.pallas import tpu as pltpu
from jax.sharding import PartitionSpec as P

F32 = jnp.float32
BF16 = jnp.bfloat16
PAD = 16
RING = 8
SLICE = 64
SCOPED = 20 * 1024 * 1024

VMEM_SPEC = pl.BlockSpec(memory_space=pltpu.VMEM)
SMEM_SPEC = pl.BlockSpec(memory_space=pltpu.SMEM)
ANY_SPEC = pl.BlockSpec(memory_space=pl.ANY)


def dot_nn(left, right):
    return lax.dot_general(left, right, (((1,), (0,)), ((), ())), preferred_element_type=F32)


def dot_nt(left, right):
    return lax.dot_general(left, right, (((1,), (1,)), ((), ())), preferred_element_type=F32)


def fold_rows(values, combine):
    parts = [values[i : i + 8] for i in range(0, values.shape[0], 8)]
    while len(parts) > 1:
        parts = [
            combine(parts[i], parts[i + 1]) if i + 1 < len(parts) else parts[i]
            for i in range(0, len(parts), 2)
        ]
    return parts[0]


def pack_places(blocks, picks, share):
    size = 2 * share + PAD
    return [
        (ref, (first + i) * size)
        for ref, (first, count) in zip(blocks, picks)
        for i in range(count)
    ]


def own_mask(at, resp):
    key_at = lax.broadcasted_iota(jnp.int32, (SLICE, resp), 0) + at
    return key_at <= lax.broadcasted_iota(jnp.int32, (SLICE, resp), 1)


def forward_kernel(heads, share, picks, after, opening, *refs):
    refs, scratch = refs[:-4], refs[-4:]
    k_all, v_all, s0, s1 = scratch
    count = len(picks)
    if opening:
        len_ref, wide_ref, own_ref = refs[:3]
        blocks = refs[3 : 3 + count]
        out_ref, e_all, g_all, q_rows, c_rows = refs[3 + count + after :]
    else:
        q_rows, c_rows = refs[:2]
        blocks = refs[2 : 2 + count]
        out_ref, e_all, g_all = refs[2 + count + after :]
    width, resp = q_rows.shape[1], q_rows.shape[0] // heads
    rate = math.log2(math.e) / math.sqrt(width)
    s_buf = (s0, s1)
    keys = k_all.shape[0]
    places = pack_places(blocks, picks, share)
    prompt = len(places) * share
    for i, (ref, at) in enumerate(places):
        k_all[i * share : (i + 1) * share, :] = ref[at : at + share, :]
        v_all[i * share : (i + 1) * share, :] = ref[at + share : at + 2 * share, :]
    if opening:
        k_all[prompt:, :] = own_ref[0]
        v_all[prompt:, :] = own_ref[1]
        live = lax.broadcasted_iota(jnp.int32, (resp, width), 0) < len_ref[0]

    for t in range(heads + 1):
        if t < heads:
            rows = slice(t * resp, (t + 1) * resp)
            if opening:
                lanes = slice(t * width, (t + 1) * width)
                q_rows[rows, :] = wide_ref[0, :, lanes]
                c_rows[rows, :] = jnp.where(live, wide_ref[1, :, lanes], jnp.zeros((), BF16))
            s_buf[t % 2][...] = dot_nt(k_all[...], q_rows[rows, :])
            g_all[:, rows] = dot_nt(v_all[...], c_rows[rows, :])
        if t > 0:
            h = t - 1
            s_now, cols = s_buf[h % 2], slice(h * resp, (h + 1) * resp)
            top = mass = mixed = None
            for at in range(0, keys, SLICE):
                s = s_now[at : at + SLICE, :]
                if at >= prompt:
                    s = jnp.where(own_mask(at - prompt, resp), s, -jnp.inf)
                part = fold_rows(s, jnp.maximum)
                top = part if top is None else jnp.maximum(top, part)
            top = jnp.max(top, axis=0, keepdims=True)
            level = top * rate
            for at in range(0, keys, SLICE):
                here = slice(at, at + SLICE)
                e = jnp.exp2(s_now[here, :] * rate - level)
                if at >= prompt:
                    e = jnp.where(own_mask(at - prompt, resp), e, 0.0)
                e_all[here, cols] = e.astype(BF16)
                part = fold_rows(e, jnp.add)
                mass = part if mass is None else mass + part
                part = fold_rows(e * g_all[here, cols], jnp.add)
                mixed = part if mixed is None else mixed + part
            out_ref[h : h + 1, :] = top
            out_ref[heads + h : heads + h + 1, :] = jnp.sum(mass, axis=0, keepdims=True)
            out_ref[2 * heads + h : 2 * heads + h + 1, :] = jnp.sum(mixed, axis=0, keepdims=True)
    paid = jnp.zeros((1, width), F32)
    for ref, at in places:
        paid = paid + ref[at + 2 * share : at + 2 * share + PAD, :].astype(F32)[:1]
    out_ref[3 * heads :, :] = jnp.broadcast_to(jnp.max(paid), (heads, resp))


def backward_kernel(heads, share, owners, picks, stats, spans, after, more, last, *refs):
    refs, (k_t, p_all, ds_all) = refs[:-3], refs[-3:]
    pay_ref, q_rows, c_rows = refs[:3]
    refs = refs[3:]
    stat_refs, refs = refs[:stats], refs[stats:]
    e_refs, g_refs, refs = refs[: len(spans)], refs[len(spans) : 2 * len(spans)], refs[2 * len(spans) :]
    blocks, refs = refs[: len(picks)], refs[len(picks) :]
    own_ref, refs = (refs[0], refs[1:]) if last else (None, refs)
    prior, refs = (refs[0], refs[1:]) if more else (None, refs)
    dq_ref, *out_refs = refs[after:]
    width, resp = q_rows.shape[1], q_rows.shape[0] // heads
    scale = 1.0 / math.sqrt(width)
    rate = scale * math.log2(math.e)

    peaks = [ref[:heads, :] for ref in stat_refs]
    peak = functools.reduce(jnp.maximum, peaks)
    weights = [jnp.exp2((local - peak) * rate) for local in peaks]
    mass, mixed, paid = 0.0, 0.0, 0.0
    for ref, weight in zip(stat_refs, weights):
        mass = mass + ref[heads : 2 * heads, :] * weight
        mixed = mixed + ref[2 * heads : 3 * heads, :] * weight
        paid = paid + ref[3 * heads :, :]
    delta = mixed / mass
    factors = [weights[group] / mass for group, _, _ in spans]
    advantage = (pay_ref[0].astype(F32) - paid / owners)[:1, :width]

    places = pack_places(blocks, picks, share)
    for i, (ref, at) in enumerate(places):
        k_t[:, i * share : (i + 1) * share] = ref[at : at + share, :].T
    prompt = len(places) * share
    if last:
        k_t[:, prompt:] = own_ref[0].T
    half = heads // 2
    dk = dv = None
    for h in range(heads):
        cols = slice(h * resp, (h + 1) * resp)
        to = 0
        for (_, first, size), e_ref, g_ref, factor in zip(spans, e_refs, g_refs, factors):
            for at in range(first, first + size, SLICE):
                p = e_ref[at : at + SLICE, cols].astype(F32) * factor[h : h + 1]
                ds = p * (g_ref[at : at + SLICE, cols] - delta[h : h + 1])
                p_all[to : to + SLICE, cols] = p.astype(BF16)
                ds_all[to : to + SLICE, cols] = ds.astype(BF16)
                to += SLICE
        lanes = slice(h * width, (h + 1) * width)
        dq = dot_nn(k_t[...], ds_all[:, cols])
        if more:
            dq = dq + prior[lanes, :]
        if last:
            dq_ref[0, :, lanes] = dq.T * (advantage * scale)
        else:
            dq_ref[lanes, :] = dq
        if h % half == half - 1:
            block = slice((h + 1 - half) * resp, (h + 1) * resp)
            dk_part = dot_nn(ds_all[:, block], q_rows[block, :])
            dv_part = dot_nn(p_all[:, block], c_rows[block, :])
            dk = dk_part if dk is None else dk + dk_part
            dv = dv_part if dv is None else dv + dv_part
    dk, dv = dk * (advantage * scale), dv * advantage
    if last:
        *out_refs, own_keys, own_values = out_refs
        own_keys[0] = dk[prompt:]
        own_values[0] = dv[prompt:]
    at = 0
    for ref in out_refs:
        for base in range(0, ref.shape[0], 2 * share):
            ref[base : base + share, :] = dk[at : at + share].astype(ref.dtype)
            ref[base + share : base + 2 * share, :] = dv[at : at + share].astype(ref.dtype)
            at += share


def forward_stats(heads, share, blocks, rows=(), opening=(), after=()):
    if opening:
        resp, width = opening[1].shape[1], blocks[0].shape[1]
        operands = (*opening, *blocks)
        specs = [SMEM_SPEC] + [VMEM_SPEC] * (len(operands) - 1)
        picks = ((0, 1),)
    else:
        resp, width = rows[0].shape[0] // heads, rows[0].shape[1]
        operands = (*rows, *blocks)
        specs = [VMEM_SPEC] * len(operands)
        picks = tuple((0, block.shape[0] // (2 * share + PAD)) for block in blocks)
    keys = share * sum(count for _, count in picks) + (resp if opening else 0)
    outs = [
        jax.ShapeDtypeStruct((4 * heads, resp), F32),
        jax.ShapeDtypeStruct((keys, heads * resp), BF16),
        jax.ShapeDtypeStruct((keys, heads * resp), F32),
    ]
    if opening:
        outs += [jax.ShapeDtypeStruct((heads * resp, width), BF16)] * 2
    return pl.pallas_call(
        functools.partial(forward_kernel, heads, share, picks, len(after), bool(opening)),
        out_shape=tuple(outs),
        in_specs=specs + [ANY_SPEC] * len(after),
        out_specs=(VMEM_SPEC,) * len(outs),
        scratch_shapes=[pltpu.VMEM((keys, width), BF16)] * 2 + [pltpu.VMEM((keys, resp), F32)] * 2,
        compiler_params=pltpu.CompilerParams(vmem_limit_bytes=SCOPED),
        cost_estimate=pl.CostEstimate(
            flops=12 * heads * resp * keys * width,
            bytes_accessed=1024 * 1024,
            transcendentals=heads * resp * keys,
        ),
        name="forward_stats",
    )(*operands, *after)


def backward_grads(
    rewards, rows, stats, kept, parts, blocks, outs, owners, heads, share, prior, after, last=()
):
    blocks, picks = [block for block, _, _ in blocks], tuple(pick for _, *pick in blocks)
    resp, width = rows[0].shape[0] // heads, rows[0].shape[1]
    more = prior is not None
    keys = sum(size for _, _, size in parts)
    dq_shape = (1, resp, heads * width) if last else (heads * width, resp)
    outs = [jax.ShapeDtypeStruct(dq_shape, F32), *outs]
    operands = (
        *rows, *stats, *(kept[g][0] for g, _, _ in parts), *(kept[g][1] for g, _, _ in parts),
        *blocks, *last, *((prior,) if more else ()),
    )
    return pl.pallas_call(
        functools.partial(
            backward_kernel, heads, share, owners, picks, len(stats), parts, len(after),
            more, bool(last),
        ),
        out_shape=tuple(outs),
        in_specs=[SMEM_SPEC] + [VMEM_SPEC] * len(operands) + [ANY_SPEC] * len(after),
        out_specs=(VMEM_SPEC,) * len(outs),
        scratch_shapes=[pltpu.VMEM((width, keys), BF16)]
        + [pltpu.VMEM((keys, heads * resp), BF16)] * 2,
        compiler_params=pltpu.CompilerParams(vmem_limit_bytes=SCOPED),
        cost_estimate=pl.CostEstimate(
            flops=20 * heads * resp * keys * width,
            bytes_accessed=2 * 1024 * 1024,
            transcendentals=0,
        ),
        name="backward_grads",
    )(rewards, *operands, *after)


def merge(part, given, first, relayed, after):
    size = part.shape[0]

    def kernel(part_ref, given_ref, relayed_ref, after_ref, out_ref):
        total = part_ref[...] + given_ref[first : first + size, :].astype(F32)
        out_ref[...] = (total + relayed_ref[...].astype(F32)).astype(BF16)

    return pl.pallas_call(
        kernel,
        out_shape=jax.ShapeDtypeStruct(part.shape, BF16),
        in_specs=[VMEM_SPEC] * 3 + [ANY_SPEC],
        out_specs=VMEM_SPEC,
        compiler_params=pltpu.CompilerParams(vmem_limit_bytes=2 * 1024 * 1024),
        cost_estimate=pl.CostEstimate(flops=0, bytes_accessed=part.size, transcendentals=0),
        name="merge",
    )(part, given, relayed, after)


def across(block):
    pairs = [(i, (i + RING) % (2 * RING)) for i in range(2 * RING)]
    return lax.ppermute(block, "sample", pairs)


def along(block, reach, side):
    partner = {}
    for start in range(math.gcd(reach, RING)):
        tour = [(start + reach * i) % RING for i in range(RING // math.gcd(reach, RING))]
        for i in range(side, len(tour) + side, 2):
            one, two = tour[i % len(tour)], tour[(i + 1) % len(tour)]
            partner[one], partner[two] = two, one
    pairs = [(y * RING + z, y * RING + partner[z]) for y in range(2) for z in range(RING)]
    return lax.ppermute(block, "sample", pairs)


def shards(queries, resp_keys, resp_values, prompt_keys, prompt_values, grad_out, lengths, rewards):
    share, width = prompt_keys.shape
    resp = queries.shape[1]
    heads = queries.shape[2] // width
    owners = lax.axis_size("sample")
    size = 2 * share
    reward_rows = jnp.broadcast_to(rewards.astype(BF16)[:, None], (PAD, width))
    packed = jnp.concatenate([prompt_keys, prompt_values, reward_rows], axis=0)
    own_rows = jnp.concatenate([resp_keys, resp_values], axis=0)
    wide_rows = jnp.concatenate([queries, grad_out], axis=0)

    def forward(*blocks, after=()):
        stat, *keep = forward_stats(heads, share, blocks, rows, after=after)
        stats.append(stat)
        kept.append(keep)

    def join(*blocks):
        return jnp.concatenate(blocks, axis=0)

    n3a, n3b, other = along(packed, 3, 0), along(packed, 3, 1), across(packed)
    both = join(packed, other)
    n2a, n2b = along(both, 2, 0), along(both, 2, 1)
    n1a, n1b = along(both, 1, 0), along(both, 1, 1)
    first, *keep, q_rows, c_rows = forward_stats(
        heads, share, [packed], opening=(lengths, wide_rows, own_rows), after=(both,)
    )
    rows, stats, kept = (q_rows, c_rows), [first], [keep]
    n4 = along(n3b, 1, 0)
    far = join(n3a, n3b, n4)
    others = across(far)
    forward(other, n3a, n3b)
    forward(n1a, n1b, after=(far,))
    forward(n2a, n2b, n4, after=(far,))
    forward(others)

    back = functools.partial(
        backward_grads, rewards, rows, stats, kept, owners=owners, heads=heads, share=share
    )
    far_ready = jax.ShapeDtypeStruct((3 * size, width), BF16)
    both_ready = jax.ShapeDtypeStruct((2 * size, width), BF16)
    wide = jax.ShapeDtypeStruct((size, width), F32)
    grads = jax.ShapeDtypeStruct((1, resp, width), F32)

    def add(part, *received):
        return sum((r.astype(F32) for r in received), part).astype(BF16)

    dq, part = back(
        ((4, 0, 3 * share),), [(others, 0, 3)], [far_ready], prior=None, after=()
    )
    given = across(part)
    dq, part_a, part_b = back(
        ((3, 0, 2 * size),), [(n2a, 0, 2), (n2b, 0, 2)], [both_ready] * 2, prior=dq, after=()
    )
    came = [along(part_a, 2, 0), along(part_b, 2, 1)]
    dq, partner, part_a, part_b, part_4 = back(
        ((1, 0, 3 * share), (3, 2 * size, share)),
        [(other, 0, 1), (n3a, 0, 1), (n3b, 0, 1), (n4, 0, 1)], [wide] * 4, prior=dq,
        after=(part_a, part_b),
    )
    part_4 = add(part_4, given[2 * size :])
    part_a = add(part_a, given[:size])
    relayed, far_a = along(part_4, 1, 0), along(part_a, 3, 0)
    dq, near_a, near_b = back(
        ((2, 0, 2 * size),), [(n1a, 0, 2), (n1b, 0, 2)], [both_ready] * 2, prior=dq,
        after=(part_4, part_a),
    )
    came += [along(near_a, 1, 0), along(near_b, 1, 1)]
    part_b = merge(part_b, given, size, relayed, near_a)
    far_b = along(part_b, 3, 1)
    grad_queries, mine, grad_resp_keys, grad_resp_values = back(
        ((0, 0, share + resp),), [(packed, 0, 1)], [wide, grads, grads], prior=dq,
        after=(part_b,), last=(own_rows,),
    )
    partner = add(partner, *(block[size:] for block in came))
    came += [far_a, far_b, across(partner)]
    total = [
        mine[at : at + share] + sum(block[at : at + share].astype(F32) for block in came)
        for at in (0, share)
    ]
    return grad_queries, grad_resp_keys, grad_resp_values, *total


def solution(mesh):
    whole = P(("problem", "sample"), None, None)
    rows = P(("problem", "sample"), None)
    one = P(("problem", "sample"))
    return jax.shard_map(
        shards,
        mesh=mesh,
        in_specs=(whole, whole, whole, rows, rows, whole, one, one),
        out_specs=(whole, whole, whole, rows, rows),
        check_vma=False,
    )
```

```python
import functools
import math

import jax
import jax.numpy as jnp
from jax import lax
from jax.experimental import pallas as pl
from jax.experimental.pallas import tpu as pltpu
from jax.sharding import PartitionSpec as P

F32 = jnp.float32
BF16 = jnp.bfloat16
PAD = 16
RING = 8
SLICE = 64
SCOPED = 20 * 1024 * 1024

VMEM_SPEC = pl.BlockSpec(memory_space=pltpu.VMEM)
SMEM_SPEC = pl.BlockSpec(memory_space=pltpu.SMEM)
ANY_SPEC = pl.BlockSpec(memory_space=pl.ANY)


def dot_nn(left, right):
    return lax.dot_general(left, right, (((1,), (0,)), ((), ())), preferred_element_type=F32)


def dot_nt(left, right):
    return lax.dot_general(left, right, (((1,), (1,)), ((), ())), preferred_element_type=F32)


def fold_rows(values, combine):
    parts = [values[i : i + 8] for i in range(0, values.shape[0], 8)]
    while len(parts) > 1:
        parts = [
            combine(parts[i], parts[i + 1]) if i + 1 < len(parts) else parts[i]
            for i in range(0, len(parts), 2)
        ]
    return parts[0]


def pack_places(blocks, share):
    size = 2 * share + PAD
    return [(ref, at) for ref in blocks for at in range(0, ref.shape[0], size)]


def load_rows(blocks, k_all, v_all, share):
    places = pack_places(blocks, share)
    for i, (ref, at) in enumerate(places):
        k_all[i * share : (i + 1) * share, :] = ref[at : at + share, :]
        v_all[i * share : (i + 1) * share, :] = ref[at + share : at + 2 * share, :]
    return len(places) * share


def own_mask(at, resp):
    key_at = lax.broadcasted_iota(jnp.int32, (SLICE, resp), 0) + at
    return key_at <= lax.broadcasted_iota(jnp.int32, (SLICE, resp), 1)


def forward_kernel(heads, share, count, opening, *refs):
    refs, scratch = refs[:-4], refs[-4:]
    k_all, v_all, s0, s1 = scratch
    if opening:
        len_ref, wide_ref, own_ref = refs[:3]
        blocks = refs[3 : 3 + count]
        out_ref, e_all, g_all, q_rows, c_rows = refs[3 + count :]
    else:
        q_rows, c_rows = refs[:2]
        blocks = refs[2 : 2 + count]
        out_ref, e_all, g_all = refs[2 + count :]
    width, resp = q_rows.shape[1], q_rows.shape[0] // heads
    rate = math.log2(math.e) / math.sqrt(width)
    s_buf = (s0, s1)
    keys = k_all.shape[0]
    prompt = load_rows(blocks, k_all, v_all, share)
    if opening:
        k_all[prompt:, :] = own_ref[0]
        v_all[prompt:, :] = own_ref[1]
        live = lax.broadcasted_iota(jnp.int32, (resp, width), 0) < len_ref[0]

    for t in range(heads + 1):
        if t < heads:
            rows = slice(t * resp, (t + 1) * resp)
            if opening:
                lanes = slice(t * width, (t + 1) * width)
                q_rows[rows, :] = wide_ref[0, :, lanes]
                c_rows[rows, :] = jnp.where(live, wide_ref[1, :, lanes], jnp.zeros((), BF16))
            s_buf[t % 2][...] = dot_nt(k_all[...], q_rows[rows, :])
            g_all[:, rows] = dot_nt(v_all[...], c_rows[rows, :])
        if t > 0:
            h = t - 1
            s_now, cols = s_buf[h % 2], slice(h * resp, (h + 1) * resp)
            top = mass = mixed = None
            for at in range(0, keys, SLICE):
                s = s_now[at : at + SLICE, :]
                if at >= prompt:
                    s = jnp.where(own_mask(at - prompt, resp), s, -jnp.inf)
                part = fold_rows(s, jnp.maximum)
                top = part if top is None else jnp.maximum(top, part)
            top = jnp.max(top, axis=0, keepdims=True)
            level = top * rate
            for at in range(0, keys, SLICE):
                here = slice(at, at + SLICE)
                e = jnp.exp2(s_now[here, :] * rate - level)
                if at >= prompt:
                    e = jnp.where(own_mask(at - prompt, resp), e, 0.0)
                e_all[here, cols] = e.astype(BF16)
                part = fold_rows(e, jnp.add)
                mass = part if mass is None else mass + part
                part = fold_rows(e * g_all[here, cols], jnp.add)
                mixed = part if mixed is None else mixed + part
            out_ref[h : h + 1, :] = top
            out_ref[heads + h : heads + h + 1, :] = jnp.sum(mass, axis=0, keepdims=True)
            out_ref[2 * heads + h : 2 * heads + h + 1, :] = jnp.sum(mixed, axis=0, keepdims=True)
    paid = jnp.zeros((1, width), F32)
    for ref, at in pack_places(blocks, share):
        paid = paid + ref[at + 2 * share : at + 2 * share + PAD, :].astype(F32)[:1]
    out_ref[3 * heads :, :] = jnp.broadcast_to(jnp.max(paid), (heads, resp))


def backward_kernel(heads, share, owners, count, stats, spans, after, more, last, *refs):
    refs, (k_t, p_all, ds_all) = refs[:-3], refs[-3:]
    pay_ref, q_rows, c_rows = refs[:3]
    refs = refs[3:]
    stat_refs, refs = refs[:stats], refs[stats:]
    e_refs, g_refs, refs = refs[: len(spans)], refs[len(spans) : 2 * len(spans)], refs[2 * len(spans) :]
    blocks, refs = refs[:count], refs[count:]
    prior, refs = (refs[0], refs[1:]) if more else (None, refs)
    dq_ref, *out_refs = refs[after:]
    width, resp = q_rows.shape[1], q_rows.shape[0] // heads
    scale = 1.0 / math.sqrt(width)
    rate = scale * math.log2(math.e)

    peaks = [ref[:heads, :] for ref in stat_refs]
    peak = functools.reduce(jnp.maximum, peaks)
    weights = [jnp.exp2((local - peak) * rate) for local in peaks]
    mass, mixed, paid = 0.0, 0.0, 0.0
    for ref, weight in zip(stat_refs, weights):
        mass = mass + ref[heads : 2 * heads, :] * weight
        mixed = mixed + ref[2 * heads : 3 * heads, :] * weight
        paid = paid + ref[3 * heads :, :]
    delta = mixed / mass
    factors = [weights[group] / mass for group, _, _ in spans]
    advantage = (pay_ref[0].astype(F32) - paid / owners)[:1, :width]

    if last:
        k_t[...] = blocks[0][0].T
    else:
        for i, (ref, at) in enumerate(pack_places(blocks, share)):
            k_t[:, i * share : (i + 1) * share] = ref[at : at + share, :].T
    half = heads // 2
    dk = dv = None
    for h in range(heads):
        cols = slice(h * resp, (h + 1) * resp)
        to = 0
        for (_, first, size), e_ref, g_ref, factor in zip(spans, e_refs, g_refs, factors):
            for at in range(first, first + size, SLICE):
                p = e_ref[at : at + SLICE, cols].astype(F32) * factor[h : h + 1]
                ds = p * (g_ref[at : at + SLICE, cols] - delta[h : h + 1])
                p_all[to : to + SLICE, cols] = p.astype(BF16)
                ds_all[to : to + SLICE, cols] = ds.astype(BF16)
                to += SLICE
        lanes = slice(h * width, (h + 1) * width)
        dq = dot_nn(k_t[...], ds_all[:, cols])
        if more:
            dq = dq + prior[lanes, :]
        if last:
            dq_ref[0, :, lanes] = dq.T * (advantage * scale)
        else:
            dq_ref[lanes, :] = dq
        if h % half == half - 1:
            block = slice((h + 1 - half) * resp, (h + 1) * resp)
            dk_part = dot_nn(ds_all[:, block], q_rows[block, :])
            dv_part = dot_nn(p_all[:, block], c_rows[block, :])
            dk = dk_part if dk is None else dk + dk_part
            dv = dv_part if dv is None else dv + dv_part
    dk, dv = dk * (advantage * scale), dv * advantage
    if last:
        out_refs[0][0] = dk
        out_refs[1][0] = dv
        return
    at = 0
    for ref in out_refs:
        for base in range(0, ref.shape[0], 2 * share):
            ref[base : base + share, :] = dk[at : at + share].astype(ref.dtype)
            ref[base + share : base + 2 * share, :] = dv[at : at + share].astype(ref.dtype)
            at += share


def forward_stats(heads, share, blocks, rows=(), opening=()):
    if opening:
        resp, width = opening[1].shape[1], opening[2].shape[2]
        operands = (*opening, *blocks)
        specs = [SMEM_SPEC] + [VMEM_SPEC] * (len(operands) - 1)
    else:
        resp, width = rows[0].shape[0] // heads, rows[0].shape[1]
        operands = (*rows, *blocks)
        specs = [VMEM_SPEC] * len(operands)
    keys = share * sum(block.shape[0] // (2 * share + PAD) for block in blocks)
    keys += resp if opening else 0
    outs = [
        jax.ShapeDtypeStruct((4 * heads, resp), F32),
        jax.ShapeDtypeStruct((keys, heads * resp), BF16),
        jax.ShapeDtypeStruct((keys, heads * resp), F32),
    ]
    if opening:
        outs += [jax.ShapeDtypeStruct((heads * resp, width), BF16)] * 2
    return pl.pallas_call(
        functools.partial(forward_kernel, heads, share, len(blocks), bool(opening)),
        out_shape=tuple(outs),
        in_specs=specs,
        out_specs=(VMEM_SPEC,) * len(outs),
        scratch_shapes=[pltpu.VMEM((keys, width), BF16)] * 2 + [pltpu.VMEM((keys, resp), F32)] * 2,
        compiler_params=pltpu.CompilerParams(vmem_limit_bytes=SCOPED),
        cost_estimate=pl.CostEstimate(
            flops=12 * heads * resp * keys * width,
            bytes_accessed=1024 * 1024,
            transcendentals=heads * resp * keys,
        ),
        name="forward_stats",
    )(*operands)


def backward_grads(
    rewards, rows, stats, kept, parts, blocks, outs, owners, heads, share, prior, after, last=False
):
    resp, width = rows[0].shape[0] // heads, rows[0].shape[1]
    more = prior is not None
    keys = sum(size for _, _, size in parts)
    dq_shape = (1, resp, heads * width) if last else (heads * width, resp)
    outs = [jax.ShapeDtypeStruct(dq_shape, F32), *outs]
    operands = (
        *rows, *stats, *(kept[g][0] for g, _, _ in parts), *(kept[g][1] for g, _, _ in parts),
        *blocks, *((prior,) if more else ()),
    )
    return pl.pallas_call(
        functools.partial(
            backward_kernel, heads, share, owners, len(blocks), len(stats), parts, len(after),
            more, last,
        ),
        out_shape=tuple(outs),
        in_specs=[SMEM_SPEC] + [VMEM_SPEC] * len(operands) + [ANY_SPEC] * len(after),
        out_specs=(VMEM_SPEC,) * len(outs),
        scratch_shapes=[pltpu.VMEM((width, keys), BF16)]
        + [pltpu.VMEM((keys, heads * resp), BF16)] * 2,
        compiler_params=pltpu.CompilerParams(vmem_limit_bytes=SCOPED),
        cost_estimate=pl.CostEstimate(
            flops=20 * heads * resp * keys * width,
            bytes_accessed=2 * 1024 * 1024,
            transcendentals=0,
        ),
        name="backward_grads",
    )(rewards, *operands, *after)


def across(block):
    pairs = [(i, (i + RING) % (2 * RING)) for i in range(2 * RING)]
    return lax.ppermute(block, "sample", pairs)


def along(block, side):
    pairs = []
    for y in range(2):
        for z in range(RING):
            other = (z + (1 if z % 2 == side else -1)) % RING
            pairs.append((y * RING + z, y * RING + other))
    return lax.ppermute(block, "sample", pairs)


def shards(queries, resp_keys, resp_values, prompt_keys, prompt_values, grad_out, lengths, rewards):
    share, width = prompt_keys.shape
    resp = queries.shape[1]
    heads = queries.shape[2] // width
    owners = lax.axis_size("sample")
    reward_rows = jnp.broadcast_to(rewards.astype(BF16)[:, None], (PAD, width))
    packed = jnp.concatenate([prompt_keys, prompt_values, reward_rows], axis=0)

    swapped = across(packed)
    wide_rows = jnp.concatenate([queries, grad_out], axis=0)
    own_rows = jnp.concatenate([resp_keys, resp_values], axis=0)
    first, *keep, q_rows, c_rows = forward_stats(
        heads, share, [packed], opening=(lengths, wide_rows, own_rows)
    )
    rows, stats, kept = (q_rows, c_rows), [first], [keep]
    both = jnp.concatenate([packed, swapped], axis=0)
    far, near = [both], [both]
    for step in (1, 2, 3, 4):
        far.append(along(far[-1], (step - 1) % 2))
        if step < 4:
            near.append(along(near[-1], step % 2))
    for blocks in ([swapped], [far[1], near[1]], [far[2], near[2]], [far[3], near[3]], [far[4]]):
        stat, *keep = forward_stats(heads, share, blocks, rows)
        stats.append(stat)
        kept.append(keep)

    back = functools.partial(
        backward_grads, rewards, rows, stats, kept, owners=owners, heads=heads, share=share
    )
    ready = jax.ShapeDtypeStruct((4 * share, width), BF16)
    wide = jax.ShapeDtypeStruct((4 * share, width), F32)
    grads = jax.ShapeDtypeStruct((1, resp, width), F32)

    def add(received, part):
        return (received.astype(F32) + part).astype(BF16)

    dq, down = back(((5, 0, 2 * share),), [far[4]], [ready], prior=None, after=())
    dq, part, up = back(
        ((4, 0, 4 * share),), [far[3], near[3]], [wide, ready], prior=dq, after=()
    )
    down = add(along(down, 1), part)
    for step in (2, 1):
        dq, part_down, part_up = back(
            ((step + 1, 0, 4 * share),), [far[step], near[step]], [wide, wide],
            prior=dq, after=(down, up),
        )
        up = add(along(up, (step + 1) % 2), part_up)
        down = add(along(down, step % 2), part_down)
    dq, mine = back(
        ((0, 0, share), (1, 0, share)), [packed, swapped], [wide], prior=dq, after=(down, up)
    )
    mine = mine + along(up, 1).astype(F32) + along(down, 0).astype(F32)
    partner = mine[2 * share :].astype(BF16)
    grad_queries, grad_resp_keys, grad_resp_values = back(
        ((0, share, resp),), [own_rows], [grads, grads], prior=dq, after=(partner,), last=True
    )
    theirs = across(partner).astype(F32)
    return (
        grad_queries, grad_resp_keys, grad_resp_values,
        mine[:share] + theirs[:share], mine[share : 2 * share] + theirs[share:],
    )


def solution(mesh):
    whole = P(("problem", "sample"), None, None)
    rows = P(("problem", "sample"), None)
    one = P(("problem", "sample"))
    return jax.shard_map(
        shards,
        mesh=mesh,
        in_specs=(whole, whole, whole, rows, rows, whole, one, one),
        out_specs=(whole, whole, whole, rows, rows),
        check_vma=False,
    )
```

```python
import functools
import math

import jax
import jax.numpy as jnp
from jax import lax
from jax.experimental import pallas as pl
from jax.experimental.pallas import tpu as pltpu
from jax.sharding import PartitionSpec as P

F32 = jnp.float32
BF16 = jnp.bfloat16
PAD = 16
RING = 8
SLICE = 64
SCOPED = 20 * 1024 * 1024

VMEM_SPEC = pl.BlockSpec(memory_space=pltpu.VMEM)
SMEM_SPEC = pl.BlockSpec(memory_space=pltpu.SMEM)
ANY_SPEC = pl.BlockSpec(memory_space=pl.ANY)


def dot_nn(left, right):
    return lax.dot_general(left, right, (((1,), (0,)), ((), ())), preferred_element_type=F32)


def dot_nt(left, right):
    return lax.dot_general(left, right, (((1,), (1,)), ((), ())), preferred_element_type=F32)


def fold_rows(values, combine):
    parts = [values[i : i + 8] for i in range(0, values.shape[0], 8)]
    while len(parts) > 1:
        parts = [
            combine(parts[i], parts[i + 1]) if i + 1 < len(parts) else parts[i]
            for i in range(0, len(parts), 2)
        ]
    return parts[0]


def pack_places(blocks, picks, share):
    size = 2 * share + PAD
    return [
        (ref, (first + i) * size)
        for ref, (first, count) in zip(blocks, picks)
        for i in range(count)
    ]


def own_mask(at, resp):
    key_at = lax.broadcasted_iota(jnp.int32, (SLICE, resp), 0) + at
    return key_at <= lax.broadcasted_iota(jnp.int32, (SLICE, resp), 1)


def forward_kernel(heads, share, picks, opening, *refs):
    refs, scratch = refs[:-4], refs[-4:]
    k_all, v_all, s0, s1 = scratch
    count = len(picks)
    if opening:
        len_ref, wide_ref, own_ref = refs[:3]
        blocks = refs[3 : 3 + count]
        out_ref, e_all, g_all, q_rows, c_rows = refs[3 + count :]
    else:
        q_rows, c_rows = refs[:2]
        blocks = refs[2 : 2 + count]
        out_ref, e_all, g_all = refs[2 + count :]
    width, resp = q_rows.shape[1], q_rows.shape[0] // heads
    rate = math.log2(math.e) / math.sqrt(width)
    s_buf = (s0, s1)
    keys = k_all.shape[0]
    places = pack_places(blocks, picks, share)
    prompt = len(places) * share
    for i, (ref, at) in enumerate(places):
        k_all[i * share : (i + 1) * share, :] = ref[at : at + share, :]
        v_all[i * share : (i + 1) * share, :] = ref[at + share : at + 2 * share, :]
    if opening:
        k_all[prompt:, :] = own_ref[0]
        v_all[prompt:, :] = own_ref[1]
        live = lax.broadcasted_iota(jnp.int32, (resp, width), 0) < len_ref[0]

    for t in range(heads + 1):
        if t < heads:
            rows = slice(t * resp, (t + 1) * resp)
            if opening:
                lanes = slice(t * width, (t + 1) * width)
                q_rows[rows, :] = wide_ref[0, :, lanes]
                c_rows[rows, :] = jnp.where(live, wide_ref[1, :, lanes], jnp.zeros((), BF16))
            s_buf[t % 2][...] = dot_nt(k_all[...], q_rows[rows, :])
            g_all[:, rows] = dot_nt(v_all[...], c_rows[rows, :])
        if t > 0:
            h = t - 1
            s_now, cols = s_buf[h % 2], slice(h * resp, (h + 1) * resp)
            top = mass = mixed = None
            for at in range(0, keys, SLICE):
                s = s_now[at : at + SLICE, :]
                if at >= prompt:
                    s = jnp.where(own_mask(at - prompt, resp), s, -jnp.inf)
                part = fold_rows(s, jnp.maximum)
                top = part if top is None else jnp.maximum(top, part)
            top = jnp.max(top, axis=0, keepdims=True)
            level = top * rate
            for at in range(0, keys, SLICE):
                here = slice(at, at + SLICE)
                e = jnp.exp2(s_now[here, :] * rate - level)
                if at >= prompt:
                    e = jnp.where(own_mask(at - prompt, resp), e, 0.0)
                e_all[here, cols] = e.astype(BF16)
                part = fold_rows(e, jnp.add)
                mass = part if mass is None else mass + part
                part = fold_rows(e * g_all[here, cols], jnp.add)
                mixed = part if mixed is None else mixed + part
            out_ref[h : h + 1, :] = top
            out_ref[heads + h : heads + h + 1, :] = jnp.sum(mass, axis=0, keepdims=True)
            out_ref[2 * heads + h : 2 * heads + h + 1, :] = jnp.sum(mixed, axis=0, keepdims=True)
    paid = jnp.zeros((1, width), F32)
    for ref, at in places:
        paid = paid + ref[at + 2 * share : at + 2 * share + PAD, :].astype(F32)[:1]
    out_ref[3 * heads :, :] = jnp.broadcast_to(jnp.max(paid), (heads, resp))


def merge_stats(stat_refs, pay_ref, merged_ref, heads, owners, width):
    rate = math.log2(math.e) / math.sqrt(width)
    peaks = [ref[:heads, :] for ref in stat_refs]
    peak = functools.reduce(jnp.maximum, peaks)
    weights = [jnp.exp2((local - peak) * rate) for local in peaks]
    mass, mixed, paid = 0.0, 0.0, 0.0
    for ref, weight in zip(stat_refs, weights):
        mass = mass + ref[heads : 2 * heads, :] * weight
        mixed = mixed + ref[2 * heads : 3 * heads, :] * weight
        paid = paid + ref[3 * heads :, :]
    for i, weight in enumerate(weights):
        merged_ref[i * heads : (i + 1) * heads, :] = weight / mass
    at = len(weights) * heads
    merged_ref[at : at + heads, :] = mixed / mass
    merged_ref[at + heads :, :] = pay_ref[0].astype(F32) - paid / owners


def backward_kernel(heads, share, owners, picks, stats, spans, after, more, last, *refs):
    refs, (k_t, p_all, ds_all) = refs[:-3], refs[-3:]
    pay_ref, q_rows, c_rows = refs[:3]
    refs = refs[3:]
    stat_refs, refs = refs[:stats], refs[stats:]
    e_refs, g_refs, refs = refs[: len(spans)], refs[len(spans) : 2 * len(spans)], refs[2 * len(spans) :]
    blocks, refs = refs[: len(picks)], refs[len(picks) :]
    own_ref, refs = (refs[0], refs[1:]) if last else (None, refs)
    prior, refs = (refs[0], refs[1:]) if more else (None, refs)
    dq_ref, *out_refs = refs[after:]
    width, resp = q_rows.shape[1], q_rows.shape[0] // heads
    scale = 1.0 / math.sqrt(width)
    if more:
        (merged_ref,) = stat_refs
    else:
        merged_ref = out_refs.pop()
        merge_stats(stat_refs, pay_ref, merged_ref, heads, owners, width)
    tail = merged_ref.shape[0] - 2 * heads
    factors = [merged_ref[group * heads : (group + 1) * heads, :] for group, _, _ in spans]
    delta = merged_ref[tail : tail + heads, :]
    advantage = merged_ref[tail + heads : tail + heads + 1, :width]

    places = pack_places(blocks, picks, share)
    for i, (ref, at) in enumerate(places):
        k_t[:, i * share : (i + 1) * share] = ref[at : at + share, :].T
    prompt = len(places) * share
    if last:
        k_t[:, prompt:] = own_ref[0].T
    ends = [heads // 2, heads - 1, heads]
    dk = dv = None
    for h in range(heads):
        cols = slice(h * resp, (h + 1) * resp)
        to = 0
        for (_, first, size), e_ref, g_ref, factor in zip(spans, e_refs, g_refs, factors):
            for at in range(first, first + size, SLICE):
                p = e_ref[at : at + SLICE, cols].astype(F32) * factor[h : h + 1]
                ds = p * (g_ref[at : at + SLICE, cols] - delta[h : h + 1])
                p_all[to : to + SLICE, cols] = p.astype(BF16)
                ds_all[to : to + SLICE, cols] = ds.astype(BF16)
                to += SLICE
        lanes = slice(h * width, (h + 1) * width)
        dq = dot_nn(k_t[...], ds_all[:, cols])
        if more:
            dq = dq + prior[lanes, :]
        if last:
            dq_ref[0, :, lanes] = dq.T * (advantage * scale)
        else:
            dq_ref[lanes, :] = dq
        if h + 1 in ends:
            block = slice(([0] + ends)[ends.index(h + 1)] * resp, (h + 1) * resp)
            dk_part = dot_nn(ds_all[:, block], q_rows[block, :])
            dv_part = dot_nn(p_all[:, block], c_rows[block, :])
            dk = dk_part if dk is None else dk + dk_part
            dv = dv_part if dv is None else dv + dv_part
    dk, dv = dk * (advantage * scale), dv * advantage
    if last:
        *out_refs, own_keys, own_values = out_refs
        own_keys[0] = dk[prompt:]
        own_values[0] = dv[prompt:]
    at = 0
    for ref in out_refs:
        for base in range(0, ref.shape[0], 2 * share):
            ref[base : base + share, :] = dk[at : at + share].astype(ref.dtype)
            ref[base + share : base + 2 * share, :] = dv[at : at + share].astype(ref.dtype)
            at += share


def forward_stats(heads, share, blocks, rows=(), opening=()):
    if opening:
        resp, width = opening[1].shape[1], blocks[0].shape[1]
        operands = (*opening, *blocks)
        specs = [SMEM_SPEC] + [VMEM_SPEC] * (len(operands) - 1)
        picks = ((0, 1),)
    else:
        resp, width = rows[0].shape[0] // heads, rows[0].shape[1]
        operands = (*rows, *blocks)
        specs = [VMEM_SPEC] * len(operands)
        picks = tuple((0, block.shape[0] // (2 * share + PAD)) for block in blocks)
    keys = share * sum(count for _, count in picks) + (resp if opening else 0)
    outs = [
        jax.ShapeDtypeStruct((4 * heads, resp), F32),
        jax.ShapeDtypeStruct((keys, heads * resp), BF16),
        jax.ShapeDtypeStruct((keys, heads * resp), F32),
    ]
    if opening:
        outs += [jax.ShapeDtypeStruct((heads * resp, width), BF16)] * 2
    return pl.pallas_call(
        functools.partial(forward_kernel, heads, share, picks, bool(opening)),
        out_shape=tuple(outs),
        in_specs=specs,
        out_specs=(VMEM_SPEC,) * len(outs),
        scratch_shapes=[pltpu.VMEM((keys, width), BF16)] * 2 + [pltpu.VMEM((keys, resp), F32)] * 2,
        compiler_params=pltpu.CompilerParams(vmem_limit_bytes=SCOPED),
        cost_estimate=pl.CostEstimate(
            flops=12 * heads * resp * keys * width,
            bytes_accessed=1024 * 1024,
            transcendentals=heads * resp * keys,
        ),
        name="forward_stats",
    )(*operands)


def backward_grads(
    rewards, rows, stats, kept, parts, blocks, outs, owners, heads, share, prior, after, last=()
):
    blocks, picks = [block for block, _, _ in blocks], tuple(pick for _, *pick in blocks)
    resp, width = rows[0].shape[0] // heads, rows[0].shape[1]
    more = prior is not None
    keys = sum(size for _, _, size in parts)
    dq_shape = (1, resp, heads * width) if last else (heads * width, resp)
    outs = [jax.ShapeDtypeStruct(dq_shape, F32), *outs]
    if not more:
        outs.append(jax.ShapeDtypeStruct(((len(stats) + 2) * heads, resp), F32))
    operands = (
        *rows, *stats, *(kept[g][0] for g, _, _ in parts), *(kept[g][1] for g, _, _ in parts),
        *blocks, *last, *((prior,) if more else ()),
    )
    return pl.pallas_call(
        functools.partial(
            backward_kernel, heads, share, owners, picks, len(stats), parts, len(after),
            more, bool(last),
        ),
        out_shape=tuple(outs),
        in_specs=[SMEM_SPEC] + [VMEM_SPEC] * len(operands) + [ANY_SPEC] * len(after),
        out_specs=(VMEM_SPEC,) * len(outs),
        scratch_shapes=[pltpu.VMEM((width, keys), BF16)]
        + [pltpu.VMEM((keys, heads * resp), BF16)] * 2,
        compiler_params=pltpu.CompilerParams(vmem_limit_bytes=SCOPED),
        cost_estimate=pl.CostEstimate(
            flops=20 * heads * resp * keys * width,
            bytes_accessed=2 * 1024 * 1024,
            transcendentals=0,
        ),
        name="backward_grads",
    )(rewards, *operands, *after)


def across(block):
    pairs = [(i, (i + RING) % (2 * RING)) for i in range(2 * RING)]
    return lax.ppermute(block, "sample", pairs)


def along(block, side):
    pairs = []
    for y in range(2):
        for z in range(RING):
            other = (z + (1 if z % 2 == side else -1)) % RING
            pairs.append((y * RING + z, y * RING + other))
    return lax.ppermute(block, "sample", pairs)


def shards(queries, resp_keys, resp_values, prompt_keys, prompt_values, grad_out, lengths, rewards):
    share, width = prompt_keys.shape
    resp = queries.shape[1]
    heads = queries.shape[2] // width
    owners = lax.axis_size("sample")
    size = 2 * share
    reward_rows = jnp.broadcast_to(rewards.astype(BF16)[:, None], (PAD, width))
    packed = jnp.concatenate([prompt_keys, prompt_values, reward_rows], axis=0)
    own_rows = jnp.concatenate([resp_keys, resp_values], axis=0)
    wide_rows = jnp.concatenate([queries, grad_out], axis=0)

    swapped = across(packed)
    first, *keep, q_rows, c_rows = forward_stats(
        heads, share, [packed], opening=(lengths, wide_rows, own_rows)
    )
    rows, stats, kept = (q_rows, c_rows), [first], [keep]
    both = jnp.concatenate([packed, swapped], axis=0)
    far, near = [both], [both]
    for step in (1, 2, 3, 4):
        far.append(along(far[-1], (step - 1) % 2))
        if step < 4:
            near.append(along(near[-1], step % 2))
    for blocks in ([swapped], [far[1], near[1]], [far[2], near[2]], [far[3], near[3]], [far[4]]):
        stat, *keep = forward_stats(heads, share, blocks, rows)
        stats.append(stat)
        kept.append(keep)

    back = functools.partial(
        backward_grads, rewards, rows, kept=kept, owners=owners, heads=heads, share=share
    )
    ready = jax.ShapeDtypeStruct((size, width), BF16)
    both_ready = jax.ShapeDtypeStruct((2 * size, width), BF16)
    wide = jax.ShapeDtypeStruct((size, width), F32)
    grads = jax.ShapeDtypeStruct((1, resp, width), F32)

    def add(part, *received):
        return sum((r.astype(F32) for r in received), part).astype(BF16)

    def planes(group, plane):
        return ((group, plane * share, share), (group, size + plane * share, share))

    dq, part, merged = back(
        stats, parts=((5, share, share),), blocks=[(far[4], 1, 1)], outs=[ready], prior=None,
        after=(),
    )
    back = functools.partial(back, (merged,))
    given = across(part)
    dq, part, part_far = back(
        parts=(*planes(4, 1), (5, 0, share)),
        blocks=[(far[3], 1, 1), (near[3], 1, 1), (far[4], 0, 1)],
        outs=[both_ready, wide], prior=dq, after=(),
    )
    down = add(part_far, given)
    given = across(part)
    up = None
    for step in (3, 2, 1):
        if step > 1:
            parts = (*planes(step, 1), *planes(step + 1, 0))
            blocks = [(far[step - 1], 1, 1), (near[step - 1], 1, 1)]
            outs = [both_ready, wide, wide]
        else:
            parts = ((1, 0, share), *planes(2, 0))
            blocks = [(swapped, 0, 1)]
            outs = [ready, wide, wide]
        blocks += [(far[step], 0, 1), (near[step], 0, 1)]
        dq, part, part_far, part_near = back(
            parts=parts, blocks=blocks, outs=outs, prior=dq,
            after=(down,) if up is None else (down, up),
        )
        relayed = () if up is None else (along(up, (step + 1) % 2),)
        up = add(part_near, given[size:], *relayed)
        down = add(part_far, given[:size], along(down, step % 2))
        given = across(part)
    grad_queries, mine, grad_resp_keys, grad_resp_values = back(
        parts=((0, 0, share + resp),), blocks=[(packed, 0, 1)], outs=[wide, grads, grads],
        prior=dq, after=(down, up), last=(own_rows,),
    )
    near, far = along(up, 1), along(down, 0)
    total = [
        mine[at : at + share] + sum(r[at : at + share].astype(F32) for r in (given, near, far))
        for at in (0, share)
    ]
    return grad_queries, grad_resp_keys, grad_resp_values, *total


def solution(mesh):
    whole = P(("problem", "sample"), None, None)
    rows = P(("problem", "sample"), None)
    one = P(("problem", "sample"))
    return jax.shard_map(
        shards,
        mesh=mesh,
        in_specs=(whole, whole, whole, rows, rows, whole, one, one),
        out_specs=(whole, whole, whole, rows, rows),
        check_vma=False,
    )
```

```python
import functools
import math

import jax
import jax.numpy as jnp
from jax import lax
from jax.experimental import pallas as pl
from jax.experimental.pallas import tpu as pltpu
from jax.sharding import PartitionSpec as P

F32 = jnp.float32
BF16 = jnp.bfloat16
PAD = 16
RING = 8
SLICE = 64
SCOPED = 20 * 1024 * 1024

VMEM_SPEC = pl.BlockSpec(memory_space=pltpu.VMEM)
SMEM_SPEC = pl.BlockSpec(memory_space=pltpu.SMEM)
ANY_SPEC = pl.BlockSpec(memory_space=pl.ANY)


def dot_nn(left, right):
    return lax.dot_general(left, right, (((1,), (0,)), ((), ())), preferred_element_type=F32)


def dot_nt(left, right):
    return lax.dot_general(left, right, (((1,), (1,)), ((), ())), preferred_element_type=F32)


def fold_rows(values, combine):
    parts = [values[i : i + 8] for i in range(0, values.shape[0], 8)]
    while len(parts) > 1:
        parts = [
            combine(parts[i], parts[i + 1]) if i + 1 < len(parts) else parts[i]
            for i in range(0, len(parts), 2)
        ]
    return parts[0]


def pack_places(blocks, picks, share):
    size = 2 * share + PAD
    return [
        (ref, (first + i) * size)
        for ref, (first, count) in zip(blocks, picks)
        for i in range(count)
    ]


def own_mask(at, size, resp):
    key_at = lax.broadcasted_iota(jnp.int32, (size, resp), 0) + at
    return key_at <= lax.broadcasted_iota(jnp.int32, (size, resp), 1)


def forward_kernel(heads, share, picks, opening, *refs):
    refs, scratch = refs[:-4], refs[-4:]
    k_all, v_all, s0, s1 = scratch
    count = len(picks)
    if opening:
        len_ref, wide_ref, own_ref = refs[:3]
        blocks = refs[3 : 3 + count]
        out_ref, e_all, g_all, q_rows, c_rows = refs[3 + count :]
    else:
        q_rows, c_rows = refs[:2]
        blocks = refs[2 : 2 + count]
        out_ref, e_all, g_all = refs[2 + count :]
    width, resp = q_rows.shape[1], q_rows.shape[0] // heads
    rate = math.log2(math.e) / math.sqrt(width)
    s_buf = (s0, s1)
    keys = k_all.shape[0]
    places = pack_places(blocks, picks, share)
    prompt = len(places) * share
    for i, (ref, at) in enumerate(places):
        k_all[i * share : (i + 1) * share, :] = ref[at : at + share, :]
        v_all[i * share : (i + 1) * share, :] = ref[at + share : at + 2 * share, :]
    if opening:
        k_all[prompt:, :] = own_ref[0]
        v_all[prompt:, :] = own_ref[1]
        live = lax.broadcasted_iota(jnp.int32, (resp, width), 0) < len_ref[0]

    tops = [None] * heads
    for t in range(heads + 1):
        h = t - 1
        if t < heads:
            rows = slice(t * resp, (t + 1) * resp)
            if opening:
                lanes = slice(t * width, (t + 1) * width)
                q_rows[rows, :] = wide_ref[0, :, lanes]
                c_rows[rows, :] = jnp.where(live, wide_ref[1, :, lanes], jnp.zeros((), BF16))
            top = None
        if t > 0:
            cols = slice(h * resp, (h + 1) * resp)
            level = tops[h] * rate
            mass = mixed = None
        for first in range(0, keys, share):
            if t < heads:
                span = slice(first, first + share)
                s = dot_nt(k_all[span, :], q_rows[rows, :])
                if first >= prompt:
                    s = jnp.where(own_mask(first - prompt, share, resp), s, -jnp.inf)
                s_buf[t % 2][span, :] = s
                part = fold_rows(s, jnp.maximum)
                top = part if top is None else jnp.maximum(top, part)
                g_all[span, rows] = dot_nt(v_all[span, :], c_rows[rows, :])
            if t > 0:
                for at in range(first, first + share, SLICE):
                    here = slice(at, at + SLICE)
                    e = jnp.exp2(s_buf[h % 2][here, :] * rate - level)
                    e_all[here, cols] = e.astype(BF16)
                    part = fold_rows(e, jnp.add)
                    mass = part if mass is None else mass + part
                    part = fold_rows(e * g_all[here, cols], jnp.add)
                    mixed = part if mixed is None else mixed + part
        if t < heads:
            tops[t] = jnp.max(top, axis=0, keepdims=True)
        if t > 0:
            out_ref[h : h + 1, :] = tops[h]
            out_ref[heads + h : heads + h + 1, :] = jnp.sum(mass, axis=0, keepdims=True)
            out_ref[2 * heads + h : 2 * heads + h + 1, :] = jnp.sum(mixed, axis=0, keepdims=True)
    paid = jnp.zeros((1, width), F32)
    for ref, at in places:
        paid = paid + ref[at + 2 * share : at + 2 * share + PAD, :].astype(F32)[:1]
    out_ref[3 * heads :, :] = jnp.broadcast_to(jnp.max(paid), (heads, resp))


def merge_stats(stat_refs, pay_ref, merged_ref, heads, owners, width):
    rate = math.log2(math.e) / math.sqrt(width)
    peaks = [ref[:heads, :] for ref in stat_refs]
    peak = functools.reduce(jnp.maximum, peaks)
    weights = [jnp.exp2((local - peak) * rate) for local in peaks]
    mass, mixed, paid = 0.0, 0.0, 0.0
    for ref, weight in zip(stat_refs, weights):
        mass = mass + ref[heads : 2 * heads, :] * weight
        mixed = mixed + ref[2 * heads : 3 * heads, :] * weight
        paid = paid + ref[3 * heads :, :]
    for i, weight in enumerate(weights):
        merged_ref[i * heads : (i + 1) * heads, :] = weight / mass
    at = len(weights) * heads
    merged_ref[at : at + heads, :] = mixed / mass
    merged_ref[at + heads :, :] = pay_ref[0].astype(F32) - paid / owners


def backward_kernel(heads, share, owners, picks, stats, spans, after, more, last, *refs):
    refs, (k_t, p_all, ds_all) = refs[:-3], refs[-3:]
    pay_ref, q_rows, c_rows = refs[:3]
    refs = refs[3:]
    stat_refs, refs = refs[:stats], refs[stats:]
    e_refs, g_refs, refs = refs[: len(spans)], refs[len(spans) : 2 * len(spans)], refs[2 * len(spans) :]
    blocks, refs = refs[: len(picks)], refs[len(picks) :]
    own_ref, refs = (refs[0], refs[1:]) if last else (None, refs)
    prior, refs = (refs[0], refs[1:]) if more else (None, refs)
    dq_ref, *out_refs = refs[after:]
    width, resp = q_rows.shape[1], q_rows.shape[0] // heads
    scale = 1.0 / math.sqrt(width)
    if more:
        (merged_ref,) = stat_refs
    else:
        merged_ref = out_refs.pop()
        merge_stats(stat_refs, pay_ref, merged_ref, heads, owners, width)
    tail = merged_ref.shape[0] - 2 * heads
    factors = [merged_ref[group * heads : (group + 1) * heads, :] for group, _, _ in spans]
    delta = merged_ref[tail : tail + heads, :]
    advantage = merged_ref[tail + heads : tail + heads + 1, :width]

    places = pack_places(blocks, picks, share)
    for i, (ref, at) in enumerate(places):
        k_t[:, i * share : (i + 1) * share] = ref[at : at + share, :].T
    prompt = len(places) * share
    if last:
        k_t[:, prompt:] = own_ref[0].T
    ends = [heads // 2, heads - 1, heads]
    dk = dv = None
    for h in range(heads):
        cols = slice(h * resp, (h + 1) * resp)
        to = 0
        for (_, first, size), e_ref, g_ref, factor in zip(spans, e_refs, g_refs, factors):
            for at in range(first, first + size, SLICE):
                p = e_ref[at : at + SLICE, cols].astype(F32) * factor[h : h + 1]
                ds = p * (g_ref[at : at + SLICE, cols] - delta[h : h + 1])
                p_all[to : to + SLICE, cols] = p.astype(BF16)
                ds_all[to : to + SLICE, cols] = ds.astype(BF16)
                to += SLICE
        lanes = slice(h * width, (h + 1) * width)
        dq = dot_nn(k_t[...], ds_all[:, cols])
        if more:
            dq = dq + prior[lanes, :]
        if last:
            dq_ref[0, :, lanes] = dq.T * (advantage * scale)
        else:
            dq_ref[lanes, :] = dq
        if h + 1 in ends:
            block = slice(([0] + ends)[ends.index(h + 1)] * resp, (h + 1) * resp)
            dk_part = dot_nn(ds_all[:, block], q_rows[block, :])
            dv_part = dot_nn(p_all[:, block], c_rows[block, :])
            dk = dk_part if dk is None else dk + dk_part
            dv = dv_part if dv is None else dv + dv_part
    dk, dv = dk * (advantage * scale), dv * advantage
    if last:
        *out_refs, own_keys, own_values = out_refs
        own_keys[0] = dk[prompt:]
        own_values[0] = dv[prompt:]
    at = 0
    for ref in out_refs:
        for base in range(0, ref.shape[0], 2 * share):
            ref[base : base + share, :] = dk[at : at + share].astype(ref.dtype)
            ref[base + share : base + 2 * share, :] = dv[at : at + share].astype(ref.dtype)
            at += share


def forward_stats(heads, share, blocks, rows=(), opening=()):
    if opening:
        resp, width = opening[1].shape[1], blocks[0].shape[1]
        operands = (*opening, *blocks)
        specs = [SMEM_SPEC] + [VMEM_SPEC] * (len(operands) - 1)
        picks = ((0, 1),)
    else:
        resp, width = rows[0].shape[0] // heads, rows[0].shape[1]
        operands = (*rows, *blocks)
        specs = [VMEM_SPEC] * len(operands)
        picks = tuple((0, block.shape[0] // (2 * share + PAD)) for block in blocks)
    keys = share * sum(count for _, count in picks) + (resp if opening else 0)
    outs = [
        jax.ShapeDtypeStruct((4 * heads, resp), F32),
        jax.ShapeDtypeStruct((keys, heads * resp), BF16),
        jax.ShapeDtypeStruct((keys, heads * resp), F32),
    ]
    if opening:
        outs += [jax.ShapeDtypeStruct((heads * resp, width), BF16)] * 2
    return pl.pallas_call(
        functools.partial(forward_kernel, heads, share, picks, bool(opening)),
        out_shape=tuple(outs),
        in_specs=specs,
        out_specs=(VMEM_SPEC,) * len(outs),
        scratch_shapes=[pltpu.VMEM((keys, width), BF16)] * 2 + [pltpu.VMEM((keys, resp), F32)] * 2,
        compiler_params=pltpu.CompilerParams(vmem_limit_bytes=SCOPED),
        cost_estimate=pl.CostEstimate(
            flops=12 * heads * resp * keys * width,
            bytes_accessed=1024 * 1024,
            transcendentals=heads * resp * keys,
        ),
        name="forward_stats",
    )(*operands)


def backward_grads(
    rewards, rows, stats, kept, parts, blocks, outs, owners, heads, share, prior, after, last=()
):
    blocks, picks = [block for block, _, _ in blocks], tuple(pick for _, *pick in blocks)
    resp, width = rows[0].shape[0] // heads, rows[0].shape[1]
    more = prior is not None
    keys = sum(size for _, _, size in parts)
    dq_shape = (1, resp, heads * width) if last else (heads * width, resp)
    outs = [jax.ShapeDtypeStruct(dq_shape, F32), *outs]
    if not more:
        outs.append(jax.ShapeDtypeStruct(((len(stats) + 2) * heads, resp), F32))
    operands = (
        *rows, *stats, *(kept[g][0] for g, _, _ in parts), *(kept[g][1] for g, _, _ in parts),
        *blocks, *last, *((prior,) if more else ()),
    )
    return pl.pallas_call(
        functools.partial(
            backward_kernel, heads, share, owners, picks, len(stats), parts, len(after),
            more, bool(last),
        ),
        out_shape=tuple(outs),
        in_specs=[SMEM_SPEC] + [VMEM_SPEC] * len(operands) + [ANY_SPEC] * len(after),
        out_specs=(VMEM_SPEC,) * len(outs),
        scratch_shapes=[pltpu.VMEM((width, keys), BF16)]
        + [pltpu.VMEM((keys, heads * resp), BF16)] * 2,
        compiler_params=pltpu.CompilerParams(vmem_limit_bytes=SCOPED),
        cost_estimate=pl.CostEstimate(
            flops=20 * heads * resp * keys * width,
            bytes_accessed=2 * 1024 * 1024,
            transcendentals=0,
        ),
        name="backward_grads",
    )(rewards, *operands, *after)


def across(block):
    pairs = [(i, (i + RING) % (2 * RING)) for i in range(2 * RING)]
    return lax.ppermute(block, "sample", pairs)


def along(block, side):
    pairs = []
    for y in range(2):
        for z in range(RING):
            other = (z + (1 if z % 2 == side else -1)) % RING
            pairs.append((y * RING + z, y * RING + other))
    return lax.ppermute(block, "sample", pairs)


def shards(queries, resp_keys, resp_values, prompt_keys, prompt_values, grad_out, lengths, rewards):
    share, width = prompt_keys.shape
    resp = queries.shape[1]
    heads = queries.shape[2] // width
    owners = lax.axis_size("sample")
    size = 2 * share
    reward_rows = jnp.broadcast_to(rewards.astype(BF16)[:, None], (PAD, width))
    packed = jnp.concatenate([prompt_keys, prompt_values, reward_rows], axis=0)
    own_rows = jnp.concatenate([resp_keys, resp_values], axis=0)
    wide_rows = jnp.concatenate([queries, grad_out], axis=0)

    swapped = across(packed)
    first, *keep, q_rows, c_rows = forward_stats(
        heads, share, [packed], opening=(lengths, wide_rows, own_rows)
    )
    rows, stats, kept = (q_rows, c_rows), [first], [keep]
    both = jnp.concatenate([packed, swapped], axis=0)
    far, near = [both], [both]
    for step in (1, 2, 3, 4):
        far.append(along(far[-1], (step - 1) % 2))
        if step < 4:
            near.append(along(near[-1], step % 2))
    for blocks in ([swapped], [far[1], near[1]], [far[2], near[2]], [far[3], near[3]], [far[4]]):
        stat, *keep = forward_stats(heads, share, blocks, rows)
        stats.append(stat)
        kept.append(keep)

    back = functools.partial(
        backward_grads, rewards, rows, kept=kept, owners=owners, heads=heads, share=share
    )
    ready = jax.ShapeDtypeStruct((2 * size, width), BF16)
    wide = jax.ShapeDtypeStruct((2 * size, width), F32)
    grads = jax.ShapeDtypeStruct((1, resp, width), F32)

    def add(part, received):
        return (received.astype(F32) + part).astype(BF16)

    dq, down, merged = back(
        stats, parts=((5, 0, size),), blocks=[(far[4], 0, 2)], outs=[ready], prior=None, after=()
    )
    back = functools.partial(back, (merged,))
    dq, part, up = back(
        parts=((4, 0, 2 * size),), blocks=[(far[3], 0, 2), (near[3], 0, 2)], outs=[wide, ready],
        prior=dq, after=(),
    )
    down = add(part, along(down, 1))
    for step in (2, 1):
        dq, part_down, part_up = back(
            parts=((step + 1, 0, 2 * size),), blocks=[(far[step], 0, 2), (near[step], 0, 2)],
            outs=[wide, wide], prior=dq, after=(down, up),
        )
        up = add(part_up, along(up, (step + 1) % 2))
        down = add(part_down, along(down, step % 2))
    dq, mine = back(
        parts=((0, 0, share), (1, 0, share)), blocks=[(packed, 0, 1), (swapped, 0, 1)],
        outs=[wide], prior=dq, after=(down, up),
    )
    mine = mine + along(up, 1).astype(F32) + along(down, 0).astype(F32)
    partner = mine[size:].astype(BF16)
    grad_queries, grad_resp_keys, grad_resp_values = back(
        parts=((0, share, resp),), blocks=[], outs=[grads, grads], prior=dq, after=(partner,),
        last=(own_rows,),
    )
    theirs = across(partner).astype(F32)
    total = [mine[at : at + share] + theirs[at : at + share] for at in (0, share)]
    return grad_queries, grad_resp_keys, grad_resp_values, *total


def solution(mesh):
    whole = P(("problem", "sample"), None, None)
    rows = P(("problem", "sample"), None)
    one = P(("problem", "sample"))
    return jax.shard_map(
        shards,
        mesh=mesh,
        in_specs=(whole, whole, whole, rows, rows, whole, one, one),
        out_specs=(whole, whole, whole, rows, rows),
        check_vma=False,
    )
```

```python
import functools
import math

import jax
import jax.numpy as jnp
from jax import lax
from jax.experimental import pallas as pl
from jax.experimental.pallas import tpu as pltpu
from jax.sharding import PartitionSpec as P

F32 = jnp.float32
BF16 = jnp.bfloat16
PAD = 16
RING = 8
SLICE = 64
SCOPED = 20 * 1024 * 1024

VMEM_SPEC = pl.BlockSpec(memory_space=pltpu.VMEM)
SMEM_SPEC = pl.BlockSpec(memory_space=pltpu.SMEM)
ANY_SPEC = pl.BlockSpec(memory_space=pl.ANY)


def dot_nn(left, right):
    return lax.dot_general(left, right, (((1,), (0,)), ((), ())), preferred_element_type=F32)


def dot_nt(left, right):
    return lax.dot_general(left, right, (((1,), (1,)), ((), ())), preferred_element_type=F32)


def fold_rows(values, combine):
    parts = [values[i : i + 8] for i in range(0, values.shape[0], 8)]
    while len(parts) > 1:
        parts = [
            combine(parts[i], parts[i + 1]) if i + 1 < len(parts) else parts[i]
            for i in range(0, len(parts), 2)
        ]
    return parts[0]


def pack_places(blocks, picks, share):
    size = 2 * share + PAD
    return [
        (ref, (first + i) * size)
        for ref, (first, count) in zip(blocks, picks)
        for i in range(count)
    ]


def own_mask(at, resp):
    key_at = lax.broadcasted_iota(jnp.int32, (SLICE, resp), 0) + at
    return key_at <= lax.broadcasted_iota(jnp.int32, (SLICE, resp), 1)


def forward_kernel(heads, share, picks, opening, *refs):
    refs, scratch = refs[:-4], refs[-4:]
    k_all, v_all, s0, s1 = scratch
    count = len(picks)
    if opening:
        len_ref, wide_ref, own_ref = refs[:3]
        blocks = refs[3 : 3 + count]
        out_ref, e_all, g_all, q_rows, c_rows = refs[3 + count :]
    else:
        q_rows, c_rows = refs[:2]
        blocks = refs[2 : 2 + count]
        out_ref, e_all, g_all = refs[2 + count :]
    width, resp = q_rows.shape[1], q_rows.shape[0] // heads
    rate = math.log2(math.e) / math.sqrt(width)
    s_buf = (s0, s1)
    keys = k_all.shape[0]
    places = pack_places(blocks, picks, share)
    prompt = len(places) * share
    for i, (ref, at) in enumerate(places):
        k_all[i * share : (i + 1) * share, :] = ref[at : at + share, :]
        v_all[i * share : (i + 1) * share, :] = ref[at + share : at + 2 * share, :]
    if opening:
        k_all[prompt:, :] = own_ref[0]
        v_all[prompt:, :] = own_ref[1]
        live = lax.broadcasted_iota(jnp.int32, (resp, width), 0) < len_ref[0]

    for t in range(heads + 1):
        if t < heads:
            rows = slice(t * resp, (t + 1) * resp)
            if opening:
                lanes = slice(t * width, (t + 1) * width)
                q_rows[rows, :] = wide_ref[0, :, lanes]
                c_rows[rows, :] = jnp.where(live, wide_ref[1, :, lanes], jnp.zeros((), BF16))
            s_buf[t % 2][...] = dot_nt(k_all[...], q_rows[rows, :])
            g_all[:, rows] = dot_nt(v_all[...], c_rows[rows, :])
        if t > 0:
            h = t - 1
            s_now, cols = s_buf[h % 2], slice(h * resp, (h + 1) * resp)
            top = mass = mixed = None
            for at in range(0, keys, SLICE):
                s = s_now[at : at + SLICE, :]
                if at >= prompt:
                    s = jnp.where(own_mask(at - prompt, resp), s, -jnp.inf)
                part = fold_rows(s, jnp.maximum)
                top = part if top is None else jnp.maximum(top, part)
            top = jnp.max(top, axis=0, keepdims=True)
            level = top * rate
            for at in range(0, keys, SLICE):
                here = slice(at, at + SLICE)
                e = jnp.exp2(s_now[here, :] * rate - level)
                if at >= prompt:
                    e = jnp.where(own_mask(at - prompt, resp), e, 0.0)
                e_all[here, cols] = e.astype(BF16)
                part = fold_rows(e, jnp.add)
                mass = part if mass is None else mass + part
                part = fold_rows(e * g_all[here, cols], jnp.add)
                mixed = part if mixed is None else mixed + part
            out_ref[h : h + 1, :] = top
            out_ref[heads + h : heads + h + 1, :] = jnp.sum(mass, axis=0, keepdims=True)
            out_ref[2 * heads + h : 2 * heads + h + 1, :] = jnp.sum(mixed, axis=0, keepdims=True)
    paid = jnp.zeros((1, width), F32)
    for ref, at in places:
        paid = paid + ref[at + 2 * share : at + 2 * share + PAD, :].astype(F32)[:1]
    out_ref[3 * heads :, :] = jnp.broadcast_to(jnp.max(paid), (heads, resp))


def merge_stats(stat_refs, pay_ref, merged_ref, heads, owners, width):
    rate = math.log2(math.e) / math.sqrt(width)
    peaks = [ref[:heads, :] for ref in stat_refs]
    peak = functools.reduce(jnp.maximum, peaks)
    weights = [jnp.exp2((local - peak) * rate) for local in peaks]
    mass, mixed, paid = 0.0, 0.0, 0.0
    for ref, weight in zip(stat_refs, weights):
        mass = mass + ref[heads : 2 * heads, :] * weight
        mixed = mixed + ref[2 * heads : 3 * heads, :] * weight
        paid = paid + ref[3 * heads :, :]
    for i, weight in enumerate(weights):
        merged_ref[i * heads : (i + 1) * heads, :] = weight / mass
    at = len(weights) * heads
    merged_ref[at : at + heads, :] = mixed / mass
    merged_ref[at + heads :, :] = pay_ref[0].astype(F32) - paid / owners


def backward_kernel(heads, share, owners, picks, stats, spans, after, more, last, *refs):
    refs, (k_t, p_all, ds_all) = refs[:-3], refs[-3:]
    pay_ref, q_rows, c_rows = refs[:3]
    refs = refs[3:]
    stat_refs, refs = refs[:stats], refs[stats:]
    e_refs, g_refs, refs = refs[: len(spans)], refs[len(spans) : 2 * len(spans)], refs[2 * len(spans) :]
    blocks, refs = refs[: len(picks)], refs[len(picks) :]
    own_ref, refs = (refs[0], refs[1:]) if last else (None, refs)
    prior, refs = (refs[0], refs[1:]) if more else (None, refs)
    dq_ref, *out_refs = refs[after:]
    width, resp = q_rows.shape[1], q_rows.shape[0] // heads
    scale = 1.0 / math.sqrt(width)
    if more:
        (merged_ref,) = stat_refs
    else:
        merged_ref = out_refs.pop()
        merge_stats(stat_refs, pay_ref, merged_ref, heads, owners, width)
    tail = merged_ref.shape[0] - 2 * heads
    factors = [merged_ref[group * heads : (group + 1) * heads, :] for group, _, _ in spans]
    delta = merged_ref[tail : tail + heads, :]
    advantage = merged_ref[tail + heads : tail + heads + 1, :width]

    places = pack_places(blocks, picks, share)
    for i, (ref, at) in enumerate(places):
        k_t[:, i * share : (i + 1) * share] = ref[at : at + share, :].T
    prompt = len(places) * share
    if last:
        k_t[:, prompt:] = own_ref[0].T
    ends = [heads // 2, heads - 1, heads]
    dk = dv = None
    for h in range(heads):
        cols = slice(h * resp, (h + 1) * resp)
        to = 0
        for (_, first, size), e_ref, g_ref, factor in zip(spans, e_refs, g_refs, factors):
            for at in range(first, first + size, SLICE):
                p = e_ref[at : at + SLICE, cols].astype(F32) * factor[h : h + 1]
                ds = p * (g_ref[at : at + SLICE, cols] - delta[h : h + 1])
                p_all[to : to + SLICE, cols] = p.astype(BF16)
                ds_all[to : to + SLICE, cols] = ds.astype(BF16)
                to += SLICE
        lanes = slice(h * width, (h + 1) * width)
        dq = dot_nn(k_t[...], ds_all[:, cols])
        if more:
            dq = dq + prior[lanes, :]
        if last:
            dq_ref[0, :, lanes] = dq.T * (advantage * scale)
        else:
            dq_ref[lanes, :] = dq
        if h + 1 in ends:
            block = slice(([0] + ends)[ends.index(h + 1)] * resp, (h + 1) * resp)
            dk_part = dot_nn(ds_all[:, block], q_rows[block, :])
            dv_part = dot_nn(p_all[:, block], c_rows[block, :])
            dk = dk_part if dk is None else dk + dk_part
            dv = dv_part if dv is None else dv + dv_part
    dk, dv = dk * (advantage * scale), dv * advantage
    if last:
        *out_refs, own_keys, own_values = out_refs
        own_keys[0] = dk[prompt:]
        own_values[0] = dv[prompt:]
    at = 0
    for ref in out_refs:
        for base in range(0, ref.shape[0], 2 * share):
            ref[base : base + share, :] = dk[at : at + share].astype(ref.dtype)
            ref[base + share : base + 2 * share, :] = dv[at : at + share].astype(ref.dtype)
            at += share


def forward_stats(heads, share, blocks, rows=(), opening=()):
    if opening:
        resp, width = opening[1].shape[1], blocks[0].shape[1]
        operands = (*opening, *blocks)
        specs = [SMEM_SPEC] + [VMEM_SPEC] * (len(operands) - 1)
        picks = ((0, 1),)
    else:
        resp, width = rows[0].shape[0] // heads, rows[0].shape[1]
        operands = (*rows, *blocks)
        specs = [VMEM_SPEC] * len(operands)
        picks = tuple((0, block.shape[0] // (2 * share + PAD)) for block in blocks)
    keys = share * sum(count for _, count in picks) + (resp if opening else 0)
    outs = [
        jax.ShapeDtypeStruct((4 * heads, resp), F32),
        jax.ShapeDtypeStruct((keys, heads * resp), BF16),
        jax.ShapeDtypeStruct((keys, heads * resp), F32),
    ]
    if opening:
        outs += [jax.ShapeDtypeStruct((heads * resp, width), BF16)] * 2
    return pl.pallas_call(
        functools.partial(forward_kernel, heads, share, picks, bool(opening)),
        out_shape=tuple(outs),
        in_specs=specs,
        out_specs=(VMEM_SPEC,) * len(outs),
        scratch_shapes=[pltpu.VMEM((keys, width), BF16)] * 2 + [pltpu.VMEM((keys, resp), F32)] * 2,
        compiler_params=pltpu.CompilerParams(vmem_limit_bytes=SCOPED),
        cost_estimate=pl.CostEstimate(
            flops=12 * heads * resp * keys * width,
            bytes_accessed=1024 * 1024,
            transcendentals=heads * resp * keys,
        ),
        name="forward_stats",
    )(*operands)


def backward_grads(
    rewards, rows, stats, kept, parts, blocks, outs, owners, heads, share, prior, after, last=()
):
    blocks, picks = [block for block, _, _ in blocks], tuple(pick for _, *pick in blocks)
    resp, width = rows[0].shape[0] // heads, rows[0].shape[1]
    more = prior is not None
    keys = sum(size for _, _, size in parts)
    dq_shape = (1, resp, heads * width) if last else (heads * width, resp)
    outs = [jax.ShapeDtypeStruct(dq_shape, F32), *outs]
    if not more:
        outs.append(jax.ShapeDtypeStruct(((len(stats) + 2) * heads, resp), F32))
    operands = (
        *rows, *stats, *(kept[g][0] for g, _, _ in parts), *(kept[g][1] for g, _, _ in parts),
        *blocks, *last, *((prior,) if more else ()),
    )
    return pl.pallas_call(
        functools.partial(
            backward_kernel, heads, share, owners, picks, len(stats), parts, len(after),
            more, bool(last),
        ),
        out_shape=tuple(outs),
        in_specs=[SMEM_SPEC] + [VMEM_SPEC] * len(operands) + [ANY_SPEC] * len(after),
        out_specs=(VMEM_SPEC,) * len(outs),
        scratch_shapes=[pltpu.VMEM((width, keys), BF16)]
        + [pltpu.VMEM((keys, heads * resp), BF16)] * 2,
        compiler_params=pltpu.CompilerParams(vmem_limit_bytes=SCOPED),
        cost_estimate=pl.CostEstimate(
            flops=20 * heads * resp * keys * width,
            bytes_accessed=2 * 1024 * 1024,
            transcendentals=0,
        ),
        name="backward_grads",
    )(rewards, *operands, *after)


def across(block):
    pairs = [(i, (i + RING) % (2 * RING)) for i in range(2 * RING)]
    return lax.ppermute(block, "sample", pairs)


def along(block, side):
    pairs = []
    for y in range(2):
        for z in range(RING):
            other = (z + (1 if z % 2 == side else -1)) % RING
            pairs.append((y * RING + z, y * RING + other))
    return lax.ppermute(block, "sample", pairs)


def shards(queries, resp_keys, resp_values, prompt_keys, prompt_values, grad_out, lengths, rewards):
    share, width = prompt_keys.shape
    resp = queries.shape[1]
    heads = queries.shape[2] // width
    owners = lax.axis_size("sample")
    size = 2 * share
    reward_rows = jnp.broadcast_to(rewards.astype(BF16)[:, None], (PAD, width))
    packed = jnp.concatenate([prompt_keys, prompt_values, reward_rows], axis=0)
    own_rows = jnp.concatenate([resp_keys, resp_values], axis=0)
    wide_rows = jnp.concatenate([queries, grad_out], axis=0)

    swapped = across(packed)
    first, *keep, q_rows, c_rows = forward_stats(
        heads, share, [packed], opening=(lengths, wide_rows, own_rows)
    )
    rows, stats, kept = (q_rows, c_rows), [first], [keep]
    both = jnp.concatenate([packed, swapped], axis=0)
    far, near = [both], [both]
    for step in (1, 2, 3, 4):
        far.append(along(far[-1], (step - 1) % 2))
        if step < 4:
            near.append(along(near[-1], step % 2))
    for blocks in ([swapped], [near[1], far[1]], [near[2], far[2]], [near[3], far[3]], [far[4]]):
        stat, *keep = forward_stats(heads, share, blocks, rows)
        stats.append(stat)
        kept.append(keep)

    back = functools.partial(
        backward_grads, rewards, rows, kept=kept, owners=owners, heads=heads, share=share
    )
    ready = jax.ShapeDtypeStruct((size, width), BF16)
    both_ready = jax.ShapeDtypeStruct((2 * size, width), BF16)
    wide = jax.ShapeDtypeStruct((size, width), F32)
    grads = jax.ShapeDtypeStruct((1, resp, width), F32)

    def add(part, *received):
        return sum((r.astype(F32) for r in received), part).astype(BF16)

    def planes(group, plane):
        return ((group, plane * share, share), (group, size + plane * share, share))

    dq, part, merged = back(
        stats, parts=((5, share, share),), blocks=[(far[4], 1, 1)], outs=[ready], prior=None,
        after=(),
    )
    back = functools.partial(back, (merged,))
    given = across(part)
    dq, part, part_far = back(
        parts=(*planes(4, 1), (5, 0, share)),
        blocks=[(near[3], 1, 1), (far[3], 1, 1), (far[4], 0, 1)],
        outs=[both_ready, wide], prior=dq, after=(),
    )
    down = add(part_far, given)
    given = across(part)
    up = None
    for step in (3, 2, 1):
        if step > 1:
            parts = (*planes(step, 1), *planes(step + 1, 0))
            blocks = [(near[step - 1], 1, 1), (far[step - 1], 1, 1)]
            outs = [both_ready, wide, wide]
        else:
            parts = ((1, 0, share), *planes(2, 0))
            blocks = [(swapped, 0, 1)]
            outs = [ready, wide, wide]
        blocks += [(near[step], 0, 1), (far[step], 0, 1)]
        dq, part, part_near, part_far = back(
            parts=parts, blocks=blocks, outs=outs, prior=dq,
            after=(down,) if up is None else (down, up),
        )
        relayed = () if up is None else (along(up, (step + 1) % 2),)
        up = add(part_near, given[:size], *relayed)
        down = add(part_far, given[size:], along(down, step % 2))
        given = across(part)
    grad_queries, mine, grad_resp_keys, grad_resp_values = back(
        parts=((0, 0, share + resp),), blocks=[(packed, 0, 1)], outs=[wide, grads, grads],
        prior=dq, after=(down, up), last=(own_rows,),
    )
    near, far = along(up, 1), along(down, 0)
    total = [
        mine[at : at + share] + sum(r[at : at + share].astype(F32) for r in (given, near, far))
        for at in (0, share)
    ]
    return grad_queries, grad_resp_keys, grad_resp_values, *total


def solution(mesh):
    whole = P(("problem", "sample"), None, None)
    rows = P(("problem", "sample"), None)
    one = P(("problem", "sample"))
    return jax.shard_map(
        shards,
        mesh=mesh,
        in_specs=(whole, whole, whole, rows, rows, whole, one, one),
        out_specs=(whole, whole, whole, rows, rows),
        check_vma=False,
    )
```
